512 devices in a mesh: row: 16 (over z, core), col: 32 (over x, y).
Axes of the slice: x: 4, y: 8, z: 8, core: 2. Of those that a mesh axis runs over, the one named last changes fastest.
Arguments:
- left_vecs: float32 [1024, 53248], P('row', 'col'), may hold values from -0.02734375 to 0.02734375
- left_cot: float32 [1024, 53248], P('row', 'col'), may hold values from -0.02734375 to 0.02734375
- right_vecs: float32 [1024, 53248], P('row', 'col'), may hold values from -0.02734375 to 0.02734375
- right_cot: float32 [1024, 53248], P('row', 'col'), may hold values from -0.02734375 to 0.02734375
- values: float32 [1024], replicated, may hold values from 0.2 to 1
- value_cot: float32 [1024], replicated, may hold values from -8 to 8
Outputs:
- slab_cot: float32 [192, 53248], P('row', 'col')
The draws below stay inside these ranges and needn't reach their ends.
All inputs are finite; a program needn't handle non-finite values.
Results may differ from the reference program's by a relative error of at most 0.000088.
Values sent between devices are 32-bit elements; how exact they have to be, the bound alone decides.
A program may use at most 64 MiB of HBM per device.

```python
import math
import jax
import jax.numpy as jnp
from jax import lax

ORDER = 53248
KEEP = 1024
SLAB = 192


def block_scale(own_key, shape, cuts, smallest, top_value):
    loudness, own = 1.0, jax.random.fold_in(own_key, 6)
    for dim, shards_of in cuts:
        steps = jnp.exp(jax.random.uniform(jax.random.fold_in(own, dim), (shards_of,), jnp.float32, smallest / len(cuts), top_value / len(cuts)))
        loudness = loudness * jnp.repeat(steps, shape[dim] // shards_of).reshape([-1 if axis == dim else 1 for axis in range(len(shape))])
    return loudness


def normal_values(stream_key, extent, scale, bound, pieces=(), held_as=jnp.bfloat16):
    factor_of = block_scale(stream_key, extent, pieces, -0.22, 0.18) if pieces else 1.0
    entries = jax.random.normal(stream_key, extent, jnp.float32) * scale * factor_of
    return jnp.minimum(jnp.maximum(entries, -bound), bound).astype(held_as)


def setup_inputs(seed: int = 0) -> dict:
    splits = jax.random.split(jax.random.key(seed), 7)
    return {
        "left_vecs": normal_values(splits[0], (KEEP, ORDER), ORDER ** -0.5, 0.02734375, ((0, 16), (1, 32)), jnp.float32),
        "left_cot": normal_values(splits[1], (KEEP, ORDER), ORDER ** -0.5, 0.02734375, ((0, 16), (1, 32)), jnp.float32),
        "right_vecs": normal_values(splits[2], (KEEP, ORDER), ORDER ** -0.5, 0.02734375, ((0, 16), (1, 32)), jnp.float32),
        "right_cot": normal_values(splits[3], (KEEP, ORDER), ORDER ** -0.5, 0.02734375, ((0, 16), (1, 32)), jnp.float32),
        "values": jnp.clip(jnp.exp(jax.random.uniform(splits[4], (KEEP,), jnp.float32, math.log(0.2), math.log(1.0))), 0.2, 1.0),
        "value_cot": normal_values(splits[5], (KEEP,), 2.0, 8.0, (), jnp.float32),
    }


broaden = 0.0001

def reference(left_vecs, left_cot, right_vecs, right_cot, values, value_cot):
    highest = lax.Precision.HIGHEST
    gram_left = jnp.dot(left_vecs, left_cot.T, precision=highest)
    gram_right = jnp.dot(right_vecs, right_cot.T, precision=highest)
    squares = values * values
    spacing = squares[None, :] - squares[:, None]
    factor = spacing / (spacing * spacing + broaden)
    inner = factor * (gram_left - gram_left.T) * values[None, :] + jnp.diag(value_cot)
    inner = inner + values[:, None] * factor * (gram_right - gram_right.T)
    mixing = inner - gram_left / values[None, :] - gram_right.T / values[:, None]
    head_left = left_vecs[:, :SLAB].T
    head_cot = left_cot[:, :SLAB].T
    first = jnp.dot(jnp.dot(head_left, mixing, precision=highest), right_vecs, precision=highest)
    second = jnp.dot(head_cot / values[None, :], right_vecs, precision=highest)
    third = jnp.dot(head_left / values[None, :], right_cot, precision=highest)
    return (first + second + third) * (ORDER / math.sqrt(KEEP))
```

```python
import functools
import math

import jax
import jax.numpy as jnp
from jax import lax
from jax.experimental import pallas as pl
from jax.experimental.pallas import tpu as pltpu
from jax.sharding import PartitionSpec as P

ORDER = 53248
KEEP = 1024
SLAB = 192
BROADEN = 0.0001
LANES = 128
F32 = jnp.float32
BF16 = jnp.bfloat16


def split(value):
    high = value.astype(BF16)
    return high, (value - high.astype(F32)).astype(BF16)


def dot_nn(left, right):
    return lax.dot_general(left, right, (((1,), (0,)), ((), ())), preferred_element_type=F32)


def dot_nt(left, right):
    return lax.dot_general(left, right, (((1,), (1,)), ((), ())), preferred_element_type=F32)


def kernel(geo, scale, *refs):
    nx, ny, nz, piece, head_piece, slab, own_cols = geo
    rows_n = 2 * nz
    plane = nx * ny
    keep = nz * LANES
    half = slab // 2
    out_rows = slab // rows_n
    width = own_cols * rows_n
    head_pieces = slab // head_piece
    groups = half // piece
    block = min(256, keep)
    (a_in, b_in, p_in, q_in, values, value_cot, out,
     panels, turned, got, lhs, rhs, p_own, p_other, column, factor,
     heads, head_own, head_x, head_extra, head_slot, head_ring, head_all,
     w_acc, w_part, w_other, rs_src, rs_buf, ar_src, ar_buf, ag_src, w_full,
     low, third, third_other, out_src, out_buf,
     load_sem, a2a_send, a2a_recv, core_send, core_recv, h1_send, h1_recv, h2_send, h2_recv,
     h3_send, h3_recv, rs_send, rs_recv, ar_send, ar_recv, ag_send, ag_recv, o_send, o_recv) = refs

    row = lax.axis_index("row")
    col = lax.axis_index("col")
    z, core = row // 2, row % 2
    x, y = col // ny, col % ny
    other = z * 2 + 1 - core
    along = (1 - core) * y + core * z
    across = (1 - core) * z + core * y
    me = x * ny + along

    def plane_device(index):
        px, pt = index // ny, index % ny
        py = (1 - core) * pt + core * y
        pz = (1 - core) * z + core * pt
        return (pz * 2 + core, px * ny + py)

    def line_device(index):
        py = (1 - core) * y + core * index
        pz = (1 - core) * index + core * z
        return (pz * 2 + core, x * ny + py)

    def remote(src, dst, send, recv, device):
        return pltpu.make_async_remote_copy(
            src_ref=src, dst_ref=dst, send_sem=send, recv_sem=recv,
            device_id=device, device_id_type=pl.DeviceIdType.MESH)

    def loop(count, step, first=0):
        def run(i, carry):
            step(i)
            return carry
        lax.fori_loop(first, count, run, 0)

    barrier = pltpu.get_barrier_semaphore()

    def greet(device):
        pl.semaphore_signal(barrier, inc=1, device_id=device, device_id_type=pl.DeviceIdType.MESH)

    loop(rows_n, lambda k: greet((lax.rem(row + k, rows_n), col)), 1)
    loop(plane, lambda k: greet(plane_device(lax.rem(me + k, plane))), 1)
    loop(nz, lambda k: greet(line_device(lax.rem(across + k, nz))), 1)

    loads = [
        pltpu.make_async_copy(source, panels.at[i // 2, pl.ds(64 * (i % 2), 64)], load_sem.at[i])
        for i, source in enumerate((a_in, b_in, p_in, q_in))
    ]
    for copy in loads:
        copy.start()
    got[:, :, own_cols:, :] = jnp.zeros((2, rows_n, LANES - own_cols, LANES), F32)

    def turn(pair):
        loads[2 * pair].wait()
        loads[2 * pair + 1].wait()
        for tile in range(width // LANES):
            turned[pair, tile * LANES:(tile + 1) * LANES, :] = panels[pair, :, tile * LANES:(tile + 1) * LANES].T

    turn(0)
    turn(1)
    pl.semaphore_wait(barrier, rows_n - 1 + plane - 1 + nz - 1)

    def a2a(pair, k):
        to = lax.rem(row + k, rows_n)
        return remote(
            turned.at[pair, pl.ds(pl.multiple_of(to * own_cols, 8), own_cols)],
            got.at[pair, row, pl.ds(0, own_cols)],
            a2a_send.at[pair, k], a2a_recv.at[pair, row], (to, col))

    def a2a_from(pair, k):
        source = lax.rem(row + k, rows_n)
        return remote(
            turned.at[pair, pl.ds(0, own_cols)], got.at[pair, source, pl.ds(0, own_cols)],
            a2a_send.at[pair, k], a2a_recv.at[pair, source], (source, col))

    first_col = col == 0
    head_core = core == 0
    carries = jnp.logical_and(head_core, col < head_pieces)
    lane = lax.broadcasted_iota(jnp.int32, (slab, LANES), 1)

    def merge(left, right, lanes):
        return (jnp.where(lanes < 64, left, pltpu.roll(right, 64, 1)),
                jnp.where(lanes < 64, pltpu.roll(left, 64, 1), right))

    to_core0 = remote(turned.at[0, pl.ds(0, slab)], head_x, core_send.at[0], core_recv.at[0], (other, col))

    def h1(p):
        return remote(head_own.at[pl.ds(pl.multiple_of(p * head_piece, 8), head_piece)], head_slot,
                      h1_send.at[p], h1_recv.at[0], (row, p))

    def h2(k):
        to = lax.rem(z + k, nz)
        return remote(head_slot, head_ring.at[z], h2_send.at[k], h2_recv.at[z], (to * 2 + core, col))

    def h2_from(k):
        source = lax.rem(z + k, nz)
        return remote(head_slot, head_ring.at[source], h2_send.at[k], h2_recv.at[source], (source * 2 + core, col))

    def head_rows(p):
        return head_all.at[:, pl.ds(pl.multiple_of(p * head_piece, 8), head_piece)]

    def h3(k):
        return remote(head_ring, head_rows(col), h3_send.at[k], h3_recv.at[col], (row, lax.rem(col + k, plane)))

    def h3_from(p):
        return remote(head_ring, head_rows(p), h3_send.at[0], h3_recv.at[p], (row, p))

    @pl.when(jnp.logical_and(first_col, core == 1))
    def _():
        to_core0.start()

    @pl.when(jnp.logical_and(first_col, head_core))
    def _():
        to_core0.wait_recv()
        head, head_cot = merge(turned[0, 0:slab, :], head_x[...], lane)
        head_own[...] = head
        here = pl.ds(pl.multiple_of(z * LANES, LANES), LANES)
        head_extra[...] = head * value_cot[:, here] + head_cot / values[:, here]
        loop(head_pieces, lambda p: h1(p).start(), 1)
        head_slot[...] = head[0:head_piece]

    loop(rows_n, lambda k: a2a(0, k).start(), 1)
    loop(rows_n, lambda k: a2a(1, k).start(), 1)
    for pair in range(2):
        got[pair, row, 0:own_cols, :] = turned[pair, pl.ds(pl.multiple_of(row * own_cols, 8), own_cols), :]

    @pl.when(carries)
    def _():
        @pl.when(jnp.logical_not(first_col))
        def _():
            h1(col).wait_recv()
        loop(nz, lambda k: h2(k).start(), 1)
        head_ring[z] = head_slot[...]

    for j in range(nz):
        here = slice(j * LANES, (j + 1) * LANES)
        column[here, :] = jnp.broadcast_to(values[:, here] * values[:, here], (LANES, LANES)).T

    def gaps(j):
        here = pl.ds(pl.multiple_of(j * LANES, LANES), LANES)
        across_values = values[:, here]
        spacing = across_values * across_values - column[...]
        factor[:, here] = spacing / (spacing * spacing + BROADEN)

    loop(nz, gaps)

    @pl.when(carries)
    def _():
        loop(nz, lambda k: h2_from(k).wait_recv(), 1)
        loop(plane, lambda k: h3(k).start(), 1)
        head_all[:, pl.ds(pl.multiple_of(col * head_piece, 8), head_piece), :] = head_ring[...]

    def prepare(pair):
        loop(rows_n, lambda k: a2a_from(pair, k).wait_recv(), 1)
        lanes = lax.broadcasted_iota(jnp.int32, (LANES, LANES), 1)
        for j in range(nz):
            first, second = merge(got[pair, 2 * j], got[pair, 2 * j + 1], lanes)
            here = slice(j * LANES, (j + 1) * LANES)
            if pair == 1:
                p_own[:, here] = first
            for at, value in ((0, second), (LANES, first)):
                high, rest = split(value)
                rhs[pair, at:at + LANES, here] = high
                rhs[pair, 256 + at:256 + at + LANES, here] = high
                rhs[pair, 512 + at:512 + at + LANES, here] = rest
            for at, value in ((0, first.T), (LANES, -second.T)):
                high, rest = split(value)
                lhs[here, at:at + LANES] = high
                lhs[here, 256 + at:256 + at + LANES] = rest
                lhs[here, 512 + at:512 + at + LANES] = high

    def through(stacked, count, high, rest, dot):
        both = dot(stacked, high)
        return both[:count] + both[count:] + dot(stacked[:count], rest)

    def low_rank(which, pair, at):
        value = through(heads[which], slab, rhs[pair, at:at + LANES, :], rhs[pair, 512 + at:512 + at + LANES, :], dot_nt)
        high, rest = split(value)
        low[0:slab, :] = high
        low[slab:, :] = rest
        return value

    def columns(pair, j):
        here = pl.ds(pl.multiple_of(j * block, block), block)
        right = rhs[pair, :, here]
        both = jnp.zeros((2 * slab, block), F32)
        total = jnp.zeros((slab, block), F32)
        for i in range(keep // block):
            there = slice(i * block, (i + 1) * block)
            high, rest = split(factor[there, here] * dot_nn(lhs[there, :], right))
            both = both + dot_nn(heads[pair, :, there], high)
            total = total + dot_nn(heads[pair, 0:slab, there], rest)
        total = total + both[:slab] + both[slab:]
        at = LANES * pair
        outer = through(low[...], slab, right[at:at + LANES], right[512 + at:512 + at + LANES], dot_nn)
        if pair == 0:
            w_acc[:, here] = total * values[:, here] - outer / values[:, here]
            return
        total = w_acc[:, here] + total - outer
        for t in range(block // LANES):
            for h in range(2):
                for g in range(groups):
                    start = h * half + g * piece
                    w_part[h, g * nz + j * (block // LANES) + t] = total[start:start + piece, t * LANES:(t + 1) * LANES]

    prepare(0)

    to_core1 = remote(head_all, head_all, core_send.at[1], core_recv.at[1], (other, col))

    @pl.when(head_core)
    def _():
        def arrived(p):
            @pl.when(p != col)
            def _():
                h3_from(p).wait_recv()
        loop(head_pieces, arrived)
        to_core1.start()

    @pl.when(core == 1)
    def _():
        to_core1.wait_recv()

    for j in range(nz):
        here = slice(j * LANES, (j + 1) * LANES)
        head = head_all[j]
        for which, value in enumerate((head, head * values[:, here], head / values[:, here])):
            high, rest = split(value)
            heads[which, 0:slab, here] = high
            heads[which, slab:, here] = rest

    low_rank(0, 0, LANES)
    loop(keep // block, functools.partial(columns, 0))
    prepare(1)
    third[...] = low_rank(2, 1, 0)
    p_swap = remote(p_own, p_other, core_send.at[2], core_recv.at[2], (other, col))
    third_swap = remote(third.at[pl.ds(pl.multiple_of((1 - core) * half, 8), half)], third_other,
                        core_send.at[3], core_recv.at[3], (other, col))
    p_swap.start()
    third_swap.start()
    loop(keep // block, functools.partial(columns, 1))

    @pl.when(jnp.logical_and(first_col, head_core))
    def _():
        for h in range(2):
            for g in range(groups):
                start = h * half + g * piece
                w_part[h, g * nz + z] = w_part[h, g * nz + z] + head_extra[start:start + piece, :]

    w_swap = remote(w_part.at[1 - core], w_other, core_send.at[4], core_recv.at[4], (other, col))
    w_swap.start()
    w_swap.wait_recv()
    rs_src[...] = w_part[core] + w_other[...]

    def rs(k):
        to = lax.rem(me + k, plane)
        return remote(rs_src.at[to], rs_buf.at[me], rs_send.at[k], rs_recv.at[me], plane_device(to))

    def rs_from(k):
        source = lax.rem(me + k, plane)
        return remote(rs_src.at[source], rs_buf.at[source], rs_send.at[k], rs_recv.at[source], plane_device(source))

    loop(plane, lambda k: rs(k).start(), 1)
    rs_buf[me] = rs_src[me]
    loop(plane, lambda k: rs_from(k).wait_recv(), 1)
    ar_src[...] = jnp.sum(rs_buf[...], axis=0)

    def ar(k):
        to = lax.rem(across + k, nz)
        return remote(ar_src, ar_buf.at[across], ar_send.at[k], ar_recv.at[across], line_device(to))

    def ar_from(k):
        source = lax.rem(across + k, nz)
        return remote(ar_src, ar_buf.at[source], ar_send.at[k], ar_recv.at[source], line_device(source))

    loop(nz, lambda k: ar(k).start(), 1)
    ar_buf[across] = ar_src[...]
    loop(nz, lambda k: ar_from(k).wait_recv(), 1)
    ag_src[...] = jnp.sum(ar_buf[...], axis=0)

    def ag(k):
        to = lax.rem(me + k, plane)
        return remote(ag_src, w_full.at[me], ag_send.at[k], ag_recv.at[me], plane_device(to))

    def ag_from(k):
        source = lax.rem(me + k, plane)
        return remote(ag_src, w_full.at[source], ag_send.at[k], ag_recv.at[source], plane_device(source))

    loop(plane, lambda k: ag(k).start(), 1)
    w_full[me] = ag_src[...]
    p_swap.wait_recv()
    third_swap.wait_recv()
    loop(plane, lambda k: ag_from(k).wait_recv(), 1)

    mine = jnp.zeros((half, LANES), F32)
    theirs = jnp.zeros((half, LANES), F32)
    for j in range(nz):
        here = slice(j * LANES, (j + 1) * LANES)
        high, rest = split(jnp.concatenate([w_full[g * nz + j] for g in range(groups)], axis=0))
        stacked = jnp.concatenate([high, rest], axis=0)
        mine = mine + through(stacked, half, rhs[1, LANES:256, here], rhs[1, 640:768, here], dot_nt)
        theirs = theirs + through(stacked, half, *split(p_other[:, here]), dot_nt)
    mine = (mine + third[pl.ds(pl.multiple_of(core * half, 8), half), :]) * scale
    theirs = (theirs + third_other[...]) * scale
    for i in range(nz):
        for at, value in ((core, mine), (1 - core, theirs)):
            out_src[i, at] = jnp.pad(value[i * out_rows:(i + 1) * out_rows], ((0, 16 - out_rows), (0, 0)))

    def send_out(i):
        to = core * nz + i
        return remote(out_src.at[i], out_buf.at[z], o_send.at[i], o_recv.at[z], (to, col))

    def out_from(i):
        source = 2 * i + row // nz
        return remote(out_src.at[i], out_buf.at[i], o_send.at[i], o_recv.at[i], (source, col))

    def each_out(step):
        def run(i):
            @pl.when(core * nz + i != row)
            def _():
                step(send_out(i))
        loop(nz, run)

    each_out(lambda copy: copy.start())

    @pl.when(core == row // nz)
    def _():
        out_buf[z] = out_src[lax.rem(row, nz)]

    def out_arrived(i):
        @pl.when(2 * i + row // nz != row)
        def _():
            out_from(i).wait_recv()
    loop(nz, out_arrived)
    for i in range(nz):
        for c in range(2):
            start = (2 * i + c) * own_cols
            out[:, start:start + own_cols] = out_buf[i, c, 0:out_rows, 0:own_cols]

    each_out(lambda copy: copy.wait_send())
    loop(rows_n, lambda k: a2a(0, k).wait_send(), 1)
    loop(rows_n, lambda k: a2a(1, k).wait_send(), 1)
    loop(plane, lambda k: rs(k).wait_send(), 1)
    loop(nz, lambda k: ar(k).wait_send(), 1)
    loop(plane, lambda k: ag(k).wait_send(), 1)
    p_swap.wait_send()
    third_swap.wait_send()
    w_swap.wait_send()

    @pl.when(jnp.logical_and(first_col, core == 1))
    def _():
        to_core0.wait_send()

    @pl.when(jnp.logical_and(first_col, head_core))
    def _():
        loop(head_pieces, lambda p: h1(p).wait_send(), 1)

    @pl.when(carries)
    def _():
        loop(nz, lambda k: h2(k).wait_send(), 1)
        loop(plane, lambda k: h3(k).wait_send(), 1)

    @pl.when(head_core)
    def _():
        to_core1.wait_send()


def body(nx, ny, nz, slab, scale, left_vecs, left_cot, right_vecs, right_cot, values, value_cot):
    rows_n, plane, keep, width = 2 * nz, nx * ny, values.shape[0], left_vecs.shape[1]
    own_cols, half = width // rows_n, slab // 2
    piece = half // (plane // nz)
    head_piece = -(-(-(-slab // plane)) // 8) * 8
    pieces = (plane, piece, LANES)
    dma = pltpu.SemaphoreType.DMA
    scratch = [
        pltpu.VMEM((2, LANES, width), F32),
        pltpu.VMEM((2, width, LANES), F32),
        pltpu.VMEM((2, rows_n, LANES, LANES), F32),
        pltpu.VMEM((keep, 768), BF16),
        pltpu.VMEM((2, 768, keep), BF16),
        pltpu.VMEM((LANES, keep), F32),
        pltpu.VMEM((LANES, keep), F32),
        pltpu.VMEM((keep, LANES), F32),
        pltpu.VMEM((keep, keep), F32),
        pltpu.VMEM((3, 2 * slab, keep), BF16),
        pltpu.VMEM((slab, LANES), F32),
        pltpu.VMEM((slab, LANES), F32),
        pltpu.VMEM((slab, LANES), F32),
        pltpu.VMEM((head_piece, LANES), F32),
        pltpu.VMEM((nz, head_piece, LANES), F32),
        pltpu.VMEM((nz, slab, LANES), F32),
        pltpu.VMEM((slab, keep), F32),
        pltpu.VMEM((2,) + pieces, F32),
        pltpu.VMEM(pieces, F32),
        pltpu.VMEM(pieces, F32),
        pltpu.VMEM(pieces, F32),
        pltpu.VMEM((piece, LANES), F32),
        pltpu.VMEM((nz, piece, LANES), F32),
        pltpu.VMEM((piece, LANES), F32),
        pltpu.VMEM(pieces, F32),
        pltpu.VMEM((2 * slab, LANES), BF16),
        pltpu.VMEM((slab, LANES), F32),
        pltpu.VMEM((half, LANES), F32),
        pltpu.VMEM((nz, 2, 16, LANES), F32),
        pltpu.VMEM((nz, 2, 16, LANES), F32),
        dma((4,)), dma((2, rows_n)), dma((2, rows_n)), dma((5,)), dma((5,)),
        dma((plane,)), dma((1,)), dma((nz,)), dma((nz,)), dma((plane,)), dma((plane,)),
        dma((plane,)), dma((plane,)), dma((nz,)), dma((nz,)), dma((plane,)), dma((plane,)),
        dma((nz,)), dma((nz,)),
    ]
    vmem, anywhere = pl.BlockSpec(memory_space=pltpu.VMEM), pl.BlockSpec(memory_space=pl.ANY)
    return pl.pallas_call(
        functools.partial(kernel, (nx, ny, nz, piece, head_piece, slab, own_cols), scale),
        out_shape=jax.ShapeDtypeStruct((slab // rows_n, width), F32),
        in_specs=[anywhere] * 4 + [vmem] * 2,
        out_specs=vmem,
        scratch_shapes=scratch,
        compiler_params=pltpu.CompilerParams(
            collective_id=0, has_side_effects=True, vmem_limit_bytes=56 * 1024 * 1024),
        cost_estimate=pl.CostEstimate(flops=12 * 2**30, bytes_accessed=2 * 2**20, transcendentals=0),
    )(left_vecs, left_cot, right_vecs, right_cot, values[None, :], value_cot[None, :])


def build(mesh, nx, ny, nz, slab, scale):
    panel = P("row", "col")
    return jax.shard_map(
        functools.partial(body, nx, ny, nz, slab, scale), mesh=mesh,
        in_specs=(panel, panel, panel, panel, P(), P()), out_specs=panel, check_vma=False)


def solution(mesh):
    return build(mesh, 4, 8, 8, SLAB, ORDER / math.sqrt(KEEP))
```

```python
import functools
import math

import jax
import jax.numpy as jnp
from jax import lax
from jax.experimental import pallas as pl
from jax.experimental.pallas import tpu as pltpu
from jax.sharding import PartitionSpec as P

ORDER = 53248
KEEP = 1024
SLAB = 192
BROADEN = 0.0001
LANES = 128
F32 = jnp.float32
BF16 = jnp.bfloat16


def split(value):
    high = value.astype(BF16)
    return high, (value - high.astype(F32)).astype(BF16)


def dot_nn(left, right):
    return lax.dot_general(left, right, (((1,), (0,)), ((), ())), preferred_element_type=F32)


def dot_nt(left, right):
    return lax.dot_general(left, right, (((1,), (1,)), ((), ())), preferred_element_type=F32)


def kernel(geo, scale, *refs):
    nx, ny, nz, piece, head_piece, slab, own_cols = geo
    rows_n = 2 * nz
    plane = nx * ny
    keep = nz * LANES
    half = slab // 2
    out_rows = slab // rows_n
    width = own_cols * rows_n
    head_pieces = slab // head_piece
    groups = half // piece
    block = min(256, keep)
    (a_in, b_in, p_in, q_in, values, value_cot, out,
     panels, turned, got, lhs, rhs, p_own, p_other, column, factor,
     heads, head_own, head_x, head_extra, head_slot, head_ring, head_all,
     w_acc, w_part, w_other, rs_src, rs_buf, ar_src, ar_buf, ag_src, w_full,
     low, third, third_other, out_src, out_buf,
     load_sem, a2a_send, a2a_recv, core_send, core_recv, h1_send, h1_recv, h2_send, h2_recv,
     h3_send, h3_recv, rs_send, rs_recv, ar_send, ar_recv, ag_send, ag_recv, o_send, o_recv) = refs

    row = lax.axis_index("row")
    col = lax.axis_index("col")
    z, core = row // 2, row % 2
    x, y = col // ny, col % ny
    other = z * 2 + 1 - core
    along = (1 - core) * y + core * z
    across = (1 - core) * z + core * y
    me = x * ny + along

    def plane_device(index):
        px, pt = index // ny, index % ny
        py = (1 - core) * pt + core * y
        pz = (1 - core) * z + core * pt
        return (pz * 2 + core, px * ny + py)

    def line_device(index):
        py = (1 - core) * y + core * index
        pz = (1 - core) * index + core * z
        return (pz * 2 + core, x * ny + py)

    def remote(src, dst, send, recv, device):
        return pltpu.make_async_remote_copy(
            src_ref=src, dst_ref=dst, send_sem=send, recv_sem=recv,
            device_id=device, device_id_type=pl.DeviceIdType.MESH)

    def loop(count, step, first=0):
        def run(i, carry):
            step(i)
            return carry
        lax.fori_loop(first, count, run, 0)

    sent = []

    def settle():
        for step in sent:
            step()

    barrier = pltpu.get_barrier_semaphore()

    def greet(device):
        pl.semaphore_signal(barrier, inc=1, device_id=device, device_id_type=pl.DeviceIdType.MESH)

    loop(rows_n, lambda k: greet((lax.rem(row + k, rows_n), col)), 1)
    loop(plane, lambda k: greet(plane_device(lax.rem(me + k, plane))), 1)
    loop(nz, lambda k: greet(line_device(lax.rem(across + k, nz))), 1)

    loads = [
        pltpu.make_async_copy(source, panels.at[i // 2, pl.ds(64 * (i % 2), 64)], load_sem.at[i])
        for i, source in enumerate((a_in, b_in, p_in, q_in))
    ]
    for copy in loads:
        copy.start()
    got[:, :, own_cols:, :] = jnp.zeros((2, rows_n, LANES - own_cols, LANES), F32)

    def turn(pair):
        loads[2 * pair].wait()
        loads[2 * pair + 1].wait()
        for tile in range(width // LANES):
            turned[pair, tile * LANES:(tile + 1) * LANES, :] = panels[pair, :, tile * LANES:(tile + 1) * LANES].T

    turn(0)
    turn(1)
    pl.semaphore_wait(barrier, rows_n - 1 + plane - 1 + nz - 1)

    def a2a(pair, k):
        to = lax.rem(row + k, rows_n)
        return remote(
            turned.at[pair, pl.ds(pl.multiple_of(to * own_cols, 8), own_cols)],
            got.at[pair, row, pl.ds(0, own_cols)],
            a2a_send.at[pair, k], a2a_recv.at[pair, row], (to, col))

    def a2a_from(pair, k):
        source = lax.rem(row + k, rows_n)
        return remote(
            turned.at[pair, pl.ds(0, own_cols)], got.at[pair, source, pl.ds(0, own_cols)],
            a2a_send.at[pair, k], a2a_recv.at[pair, source], (source, col))

    first_col = col == 0
    head_core = core == 0
    carries = jnp.logical_and(head_core, col < head_pieces)
    lane = lax.broadcasted_iota(jnp.int32, (slab, LANES), 1)

    def merge(left, right, lanes):
        return (jnp.where(lanes < 64, left, pltpu.roll(right, 64, 1)),
                jnp.where(lanes < 64, pltpu.roll(left, 64, 1), right))

    to_core0 = remote(turned.at[0, pl.ds(0, slab)], head_x, core_send.at[0], core_recv.at[0], (other, col))

    def h1(p):
        return remote(head_own.at[pl.ds(pl.multiple_of(p * head_piece, 8), head_piece)], head_slot,
                      h1_send.at[p], h1_recv.at[0], (row, p))

    def h2(k):
        to = lax.rem(z + k, nz)
        return remote(head_slot, head_ring.at[z], h2_send.at[k], h2_recv.at[z], (to * 2 + core, col))

    def h2_from(k):
        source = lax.rem(z + k, nz)
        return remote(head_slot, head_ring.at[source], h2_send.at[k], h2_recv.at[source], (source * 2 + core, col))

    def head_rows(p):
        return head_all.at[:, pl.ds(pl.multiple_of(p * head_piece, 8), head_piece)]

    def h3(k):
        return remote(head_ring, head_rows(col), h3_send.at[k], h3_recv.at[col], (row, lax.rem(col + k, plane)))

    def h3_from(p):
        return remote(head_ring, head_rows(p), h3_send.at[0], h3_recv.at[p], (row, p))

    far_first = [half_way + sign * step for half_way in (rows_n // 2,) for step in range(half_way) for sign in (1, -1)]
    far_first = [k for i, k in enumerate(far_first) if k not in far_first[:i]]
    order = [(pair, k) for pair in range(2) for k in far_first]
    window = min(6, len(far_first) // 2)

    def issue(first, last):
        for i in range(first, min(last, len(order))):
            if window <= i < 2 * window:
                a2a(*order[i - window]).wait_send()
            a2a(*order[i]).start()

    @pl.when(jnp.logical_and(first_col, core == 1))
    def _():
        to_core0.start()

    issue(0, window)

    @pl.when(jnp.logical_and(first_col, head_core))
    def _():
        to_core0.wait_recv()
        head, head_cot = merge(turned[0, 0:slab, :], head_x[...], lane)
        head_own[...] = head
        here = pl.ds(pl.multiple_of(z * LANES, LANES), LANES)
        head_extra[...] = head * value_cot[:, here] + head_cot / values[:, here]
        loop(head_pieces, lambda p: h1(p).start(), 1)
        head_slot[...] = head[0:head_piece]

    @pl.when(jnp.logical_and(first_col, core == 1))
    def _():
        to_core0.wait_send()

    for pair in range(2):
        got[pair, row, 0:own_cols, :] = turned[pair, pl.ds(pl.multiple_of(row * own_cols, 8), own_cols), :]

    @pl.when(carries)
    def _():
        @pl.when(jnp.logical_not(first_col))
        def _():
            h1(col).wait_recv()
        loop(nz, lambda k: h2(k).start(), 1)
        head_ring[z] = head_slot[...]

    issue(window, 2 * window)

    @pl.when(carries)
    def _():
        loop(nz, lambda k: h2_from(k).wait_recv(), 1)
        loop(plane, lambda k: h3(k).start(), 1)
        head_all[:, pl.ds(pl.multiple_of(col * head_piece, 8), head_piece), :] = head_ring[...]

    issue(2 * window, len(order))

    def a2a_sent():
        for item in order[window:]:
            a2a(*item).wait_send()

    sent.append(a2a_sent)

    for j in range(nz):
        here = slice(j * LANES, (j + 1) * LANES)
        column[here, :] = jnp.broadcast_to(values[:, here] * values[:, here], (LANES, LANES)).T

    def gaps(j):
        here = pl.ds(pl.multiple_of(j * LANES, LANES), LANES)
        across_values = values[:, here]
        spacing = across_values * across_values - column[...]
        factor[:, here] = spacing / (spacing * spacing + BROADEN)

    loop(nz, gaps)

    def head_sent():
        @pl.when(jnp.logical_and(first_col, head_core))
        def _():
            loop(head_pieces, lambda p: h1(p).wait_send(), 1)

        @pl.when(carries)
        def _():
            loop(nz, lambda k: h2(k).wait_send(), 1)
            loop(plane, lambda k: h3(k).wait_send(), 1)

    sent.append(head_sent)

    def prepare(pair):
        loop(rows_n, lambda k: a2a_from(pair, k).wait_recv(), 1)
        lanes = lax.broadcasted_iota(jnp.int32, (LANES, LANES), 1)
        for j in range(nz):
            first, second = merge(got[pair, 2 * j], got[pair, 2 * j + 1], lanes)
            here = slice(j * LANES, (j + 1) * LANES)
            if pair == 1:
                p_own[:, here] = first
            for at, value in ((0, second), (LANES, first)):
                high, rest = split(value)
                rhs[pair, at:at + LANES, here] = high
                rhs[pair, 256 + at:256 + at + LANES, here] = high
                rhs[pair, 512 + at:512 + at + LANES, here] = rest
            for at, value in ((0, first.T), (LANES, -second.T)):
                high, rest = split(value)
                lhs[here, at:at + LANES] = high
                lhs[here, 256 + at:256 + at + LANES] = rest
                lhs[here, 512 + at:512 + at + LANES] = high

    def through(stacked, count, high, rest, dot):
        both = dot(stacked, high)
        return both[:count] + both[count:] + dot(stacked[:count], rest)

    def low_rank(which, pair, at):
        value = through(heads[which], slab, rhs[pair, at:at + LANES, :], rhs[pair, 512 + at:512 + at + LANES, :], dot_nt)
        high, rest = split(value)
        low[0:slab, :] = high
        low[slab:, :] = rest
        return value

    def columns(pair, j):
        here = pl.ds(pl.multiple_of(j * block, block), block)
        right = rhs[pair, :, here]
        both = jnp.zeros((2 * slab, block), F32)
        total = jnp.zeros((slab, block), F32)
        for i in range(keep // block):
            there = slice(i * block, (i + 1) * block)
            high, rest = split(factor[there, here] * dot_nn(lhs[there, :], right))
            both = both + dot_nn(heads[pair, :, there], high)
            total = total + dot_nn(heads[pair, 0:slab, there], rest)
        total = total + both[:slab] + both[slab:]
        at = LANES * pair
        outer = through(low[...], slab, right[at:at + LANES], right[512 + at:512 + at + LANES], dot_nn)
        if pair == 0:
            w_acc[:, here] = total * values[:, here] - outer / values[:, here]
            return
        total = w_acc[:, here] + total - outer
        for t in range(block // LANES):
            for h in range(2):
                for g in range(groups):
                    start = h * half + g * piece
                    w_part[h, g * nz + j * (block // LANES) + t] = total[start:start + piece, t * LANES:(t + 1) * LANES]

    prepare(0)

    to_core1 = remote(head_all, head_all, core_send.at[1], core_recv.at[1], (other, col))

    @pl.when(head_core)
    def _():
        def arrived(p):
            @pl.when(p != col)
            def _():
                h3_from(p).wait_recv()
        loop(head_pieces, arrived)
        to_core1.start()

    @pl.when(core == 1)
    def _():
        to_core1.wait_recv()

    def head_core_sent():
        @pl.when(head_core)
        def _():
            to_core1.wait_send()

    sent.append(head_core_sent)

    for j in range(nz):
        here = slice(j * LANES, (j + 1) * LANES)
        head = head_all[j]
        for which, value in enumerate((head, head * values[:, here], head / values[:, here])):
            high, rest = split(value)
            heads[which, 0:slab, here] = high
            heads[which, slab:, here] = rest

    low_rank(0, 0, LANES)
    loop(keep // block, functools.partial(columns, 0))
    prepare(1)
    third[...] = low_rank(2, 1, 0)
    p_swap = remote(p_own, p_other, core_send.at[2], core_recv.at[2], (other, col))
    third_swap = remote(third.at[pl.ds(pl.multiple_of((1 - core) * half, 8), half)], third_other,
                        core_send.at[3], core_recv.at[3], (other, col))
    p_swap.start()
    third_swap.start()
    sent.extend((p_swap.wait_send, third_swap.wait_send))
    loop(keep // block, functools.partial(columns, 1))

    @pl.when(jnp.logical_and(first_col, head_core))
    def _():
        for h in range(2):
            for g in range(groups):
                start = h * half + g * piece
                w_part[h, g * nz + z] = w_part[h, g * nz + z] + head_extra[start:start + piece, :]

    w_swap = remote(w_part.at[1 - core], w_other, core_send.at[4], core_recv.at[4], (other, col))
    w_swap.start()
    sent.append(w_swap.wait_send)
    w_swap.wait_recv()
    rs_src[...] = w_part[core] + w_other[...]

    def rs(k):
        to = lax.rem(me + k, plane)
        return remote(rs_src.at[to], rs_buf.at[me], rs_send.at[k], rs_recv.at[me], plane_device(to))

    def rs_from(k):
        source = lax.rem(me + k, plane)
        return remote(rs_src.at[source], rs_buf.at[source], rs_send.at[k], rs_recv.at[source], plane_device(source))

    loop(plane, lambda k: rs(k).start(), 1)
    sent.append(lambda: loop(plane, lambda k: rs(k).wait_send(), 1))
    rs_buf[me] = rs_src[me]
    loop(plane, lambda k: rs_from(k).wait_recv(), 1)
    ar_src[...] = jnp.sum(rs_buf[...], axis=0)

    def ar(k):
        to = lax.rem(across + k, nz)
        return remote(ar_src, ar_buf.at[across], ar_send.at[k], ar_recv.at[across], line_device(to))

    def ar_from(k):
        source = lax.rem(across + k, nz)
        return remote(ar_src, ar_buf.at[source], ar_send.at[k], ar_recv.at[source], line_device(source))

    loop(nz, lambda k: ar(k).start(), 1)
    sent.append(lambda: loop(nz, lambda k: ar(k).wait_send(), 1))
    ar_buf[across] = ar_src[...]
    loop(nz, lambda k: ar_from(k).wait_recv(), 1)
    ag_src[...] = jnp.sum(ar_buf[...], axis=0)

    def ag(k):
        to = lax.rem(me + k, plane)
        return remote(ag_src, w_full.at[me], ag_send.at[k], ag_recv.at[me], plane_device(to))

    def ag_from(k):
        source = lax.rem(me + k, plane)
        return remote(ag_src, w_full.at[source], ag_send.at[k], ag_recv.at[source], plane_device(source))

    loop(plane, lambda k: ag(k).start(), 1)
    sent.append(lambda: loop(plane, lambda k: ag(k).wait_send(), 1))
    w_full[me] = ag_src[...]
    p_swap.wait_recv()
    third_swap.wait_recv()
    loop(plane, lambda k: ag_from(k).wait_recv(), 1)

    mine = jnp.zeros((half, LANES), F32)
    theirs = jnp.zeros((half, LANES), F32)
    for j in range(nz):
        here = slice(j * LANES, (j + 1) * LANES)
        high, rest = split(jnp.concatenate([w_full[g * nz + j] for g in range(groups)], axis=0))
        stacked = jnp.concatenate([high, rest], axis=0)
        mine = mine + through(stacked, half, rhs[1, LANES:256, here], rhs[1, 640:768, here], dot_nt)
        theirs = theirs + through(stacked, half, *split(p_other[:, here]), dot_nt)
    mine = (mine + third[pl.ds(pl.multiple_of(core * half, 8), half), :]) * scale
    theirs = (theirs + third_other[...]) * scale
    for i in range(nz):
        for at, value in ((core, mine), (1 - core, theirs)):
            out_src[i, at] = jnp.pad(value[i * out_rows:(i + 1) * out_rows], ((0, 16 - out_rows), (0, 0)))

    def send_out(i):
        to = core * nz + i
        return remote(out_src.at[i], out_buf.at[z], o_send.at[i], o_recv.at[z], (to, col))

    def out_from(i):
        source = 2 * i + row // nz
        return remote(out_src.at[i], out_buf.at[i], o_send.at[i], o_recv.at[i], (source, col))

    def each_out(step):
        def run(i):
            @pl.when(core * nz + i != row)
            def _():
                step(send_out(i))
        loop(nz, run)

    each_out(lambda copy: copy.start())

    @pl.when(core == row // nz)
    def _():
        out_buf[z] = out_src[lax.rem(row, nz)]

    def out_arrived(i):
        @pl.when(2 * i + row // nz != row)
        def _():
            out_from(i).wait_recv()
    loop(nz, out_arrived)
    for i in range(nz):
        for c in range(2):
            start = (2 * i + c) * own_cols
            out[:, start:start + own_cols] = out_buf[i, c, 0:out_rows, 0:own_cols]

    each_out(lambda copy: copy.wait_send())
    settle()


def body(nx, ny, nz, slab, scale, left_vecs, left_cot, right_vecs, right_cot, values, value_cot):
    rows_n, plane, keep, width = 2 * nz, nx * ny, values.shape[0], left_vecs.shape[1]
    own_cols, half = width // rows_n, slab // 2
    piece = half // (plane // nz)
    head_piece = -(-(-(-slab // plane)) // 8) * 8
    pieces = (plane, piece, LANES)
    dma = pltpu.SemaphoreType.DMA
    scratch = [
        pltpu.VMEM((2, LANES, width), F32),
        pltpu.VMEM((2, width, LANES), F32),
        pltpu.VMEM((2, rows_n, LANES, LANES), F32),
        pltpu.VMEM((keep, 768), BF16),
        pltpu.VMEM((2, 768, keep), BF16),
        pltpu.VMEM((LANES, keep), F32),
        pltpu.VMEM((LANES, keep), F32),
        pltpu.VMEM((keep, LANES), F32),
        pltpu.VMEM((keep, keep), F32),
        pltpu.VMEM((3, 2 * slab, keep), BF16),
        pltpu.VMEM((slab, LANES), F32),
        pltpu.VMEM((slab, LANES), F32),
        pltpu.VMEM((slab, LANES), F32),
        pltpu.VMEM((head_piece, LANES), F32),
        pltpu.VMEM((nz, head_piece, LANES), F32),
        pltpu.VMEM((nz, slab, LANES), F32),
        pltpu.VMEM((slab, keep), F32),
        pltpu.VMEM((2,) + pieces, F32),
        pltpu.VMEM(pieces, F32),
        pltpu.VMEM(pieces, F32),
        pltpu.VMEM(pieces, F32),
        pltpu.VMEM((piece, LANES), F32),
        pltpu.VMEM((nz, piece, LANES), F32),
        pltpu.VMEM((piece, LANES), F32),
        pltpu.VMEM(pieces, F32),
        pltpu.VMEM((2 * slab, LANES), BF16),
        pltpu.VMEM((slab, LANES), F32),
        pltpu.VMEM((half, LANES), F32),
        pltpu.VMEM((nz, 2, 16, LANES), F32),
        pltpu.VMEM((nz, 2, 16, LANES), F32),
        dma((4,)), dma((2, rows_n)), dma((2, rows_n)), dma((5,)), dma((5,)),
        dma((plane,)), dma((1,)), dma((nz,)), dma((nz,)), dma((plane,)), dma((plane,)),
        dma((plane,)), dma((plane,)), dma((nz,)), dma((nz,)), dma((plane,)), dma((plane,)),
        dma((nz,)), dma((nz,)),
    ]
    vmem, anywhere = pl.BlockSpec(memory_space=pltpu.VMEM), pl.BlockSpec(memory_space=pl.ANY)
    return pl.pallas_call(
        functools.partial(kernel, (nx, ny, nz, piece, head_piece, slab, own_cols), scale),
        out_shape=jax.ShapeDtypeStruct((slab // rows_n, width), F32),
        in_specs=[anywhere] * 4 + [vmem] * 2,
        out_specs=vmem,
        scratch_shapes=scratch,
        compiler_params=pltpu.CompilerParams(
            collective_id=0, has_side_effects=True, vmem_limit_bytes=56 * 1024 * 1024),
        cost_estimate=pl.CostEstimate(flops=12 * 2**30, bytes_accessed=2 * 2**20, transcendentals=0),
    )(left_vecs, left_cot, right_vecs, right_cot, values[None, :], value_cot[None, :])


def build(mesh, nx, ny, nz, slab, scale):
    panel = P("row", "col")
    return jax.shard_map(
        functools.partial(body, nx, ny, nz, slab, scale), mesh=mesh,
        in_specs=(panel, panel, panel, panel, P(), P()), out_specs=panel, check_vma=False)


def solution(mesh):
    return build(mesh, 4, 8, 8, SLAB, ORDER / math.sqrt(KEEP))
```

```python
import functools
import math

import jax
import jax.numpy as jnp
from jax import lax
from jax.experimental import pallas as pl
from jax.experimental.pallas import tpu as pltpu
from jax.sharding import PartitionSpec as P

ORDER = 53248
KEEP = 1024
SLAB = 192
BROADEN = 0.0001
LANES = 128
F32 = jnp.float32
BF16 = jnp.bfloat16


def split(value):
    high = value.astype(BF16)
    return high, (value - high.astype(F32)).astype(BF16)


def dot_nn(left, right):
    return lax.dot_general(left, right, (((1,), (0,)), ((), ())), preferred_element_type=F32)


def dot_nt(left, right):
    return lax.dot_general(left, right, (((1,), (1,)), ((), ())), preferred_element_type=F32)


def kernel(geo, *refs):
    nx, ny, nz, piece, head_piece, slab, own_cols = geo
    rows_n = 2 * nz
    plane = nx * ny
    keep = nz * LANES
    half = slab // 2
    out_rows = slab // rows_n
    width = own_cols * rows_n
    head_pieces = slab // head_piece
    groups = half // piece
    block = keep // 2
    (a_in, b_in, p_in, q_in, values, value_cot, out,
     panels, turned, got, lhs, rhs, p_own, p_other, column, factor,
     heads, head_own, head_x, head_extra, head_slot, head_ring, head_all,
     w_acc, w_part, w_other, rs_src, rs_buf, ar_src, ar_buf, ag_src, w_full,
     sym_high, sym_rest, low, third, third_other, out_src, out_buf,
     load_sem, a2a_send, a2a_recv, core_send, core_recv, h1_send, h1_recv, h2_send, h2_recv,
     h3_send, h3_recv, rs_send, rs_recv, ar_send, ar_recv, ag_send, ag_recv, o_send, o_recv) = refs

    row = lax.axis_index("row")
    col = lax.axis_index("col")
    z, core = row // 2, row % 2
    x, y = col // ny, col % ny
    other = z * 2 + 1 - core
    along = (1 - core) * y + core * z
    across = (1 - core) * z + core * y
    me = x * ny + along

    def plane_device(index):
        px, pt = index // ny, index % ny
        py = (1 - core) * pt + core * y
        pz = (1 - core) * z + core * pt
        return (pz * 2 + core, px * ny + py)

    def line_device(index):
        py = (1 - core) * y + core * index
        pz = (1 - core) * index + core * z
        return (pz * 2 + core, x * ny + py)

    def remote(src, dst, send, recv, device):
        return pltpu.make_async_remote_copy(
            src_ref=src, dst_ref=dst, send_sem=send, recv_sem=recv,
            device_id=device, device_id_type=pl.DeviceIdType.MESH)

    def loop(count, step, first=0):
        def run(i, carry):
            step(i)
            return carry
        lax.fori_loop(first, count, run, 0)

    line_order = sorted(range(1, nz), key=lambda d: -min(d, nz - d))
    plane_order = sorted(
        ((dx, dt) for dx in range(nx) for dt in range(ny) if dx or dt),
        key=lambda at: -min(at[0], nx - at[0]) - min(at[1], ny - at[1]))
    row_order = [(0, 0)] + [(d, c) for d in line_order for c in range(2)]

    def around(dx, dt):
        return lax.rem(x + dx, nx) * ny + lax.rem(along + dt, ny)

    def row_target(d, c):
        return lax.rem(z + d, nz) * 2 + c if d else other

    sent = []

    def settle():
        for step in sent:
            step()

    barrier = pltpu.get_barrier_semaphore()

    def greet(device):
        pl.semaphore_signal(barrier, inc=1, device_id=device, device_id_type=pl.DeviceIdType.MESH)

    for dx, dt in plane_order:
        greet(plane_device(around(dx, dt)))
    for d in line_order:
        greet(line_device(lax.rem(across + d, nz)))
    for d, c in row_order:
        greet((row_target(d, c), col))

    loads = [
        pltpu.make_async_copy(source, panels.at[i // 2, pl.ds(64 * (i % 2), 64)], load_sem.at[i])
        for i, source in enumerate((a_in, b_in, p_in, q_in))
    ]
    for copy in loads:
        copy.start()
    got[:, :, own_cols:, :] = jnp.zeros((2, rows_n, LANES - own_cols, LANES), F32)

    def turn(pair):
        loads[2 * pair].wait()
        loads[2 * pair + 1].wait()
        for tile in range(width // LANES):
            turned[pair, tile * LANES:(tile + 1) * LANES, :] = panels[pair, :, tile * LANES:(tile + 1) * LANES].T

    turn(0)
    turn(1)
    pl.semaphore_wait(barrier, rows_n - 1 + plane - 1 + nz - 1)

    def a2a(pair, d, c):
        to = row_target(d, c)
        return remote(
            turned.at[pair, pl.ds(pl.multiple_of(to * own_cols, 8), own_cols)],
            got.at[pair, row, pl.ds(0, own_cols)],
            a2a_send.at[pair, 2 * d + c], a2a_recv.at[pair, row], (to, col))

    def a2a_from(pair, source):
        return remote(
            turned.at[pair, pl.ds(0, own_cols)], got.at[pair, source, pl.ds(0, own_cols)],
            a2a_send.at[pair, 0], a2a_recv.at[pair, source], (source, col))

    first_col = col == 0
    head_core = core == 0
    carries = jnp.logical_and(head_core, col < head_pieces)
    lane = lax.broadcasted_iota(jnp.int32, (slab, LANES), 1)

    def merge(left, right, lanes):
        return (jnp.where(lanes < 64, left, pltpu.roll(right, 64, 1)),
                jnp.where(lanes < 64, pltpu.roll(left, 64, 1), right))

    to_core0 = remote(turned.at[0, pl.ds(0, slab)], head_x, core_send.at[0], core_recv.at[0], (other, col))

    def h1(p):
        return remote(head_own.at[pl.ds(pl.multiple_of(p * head_piece, 8), head_piece)], head_slot,
                      h1_send.at[p], h1_recv.at[0], (row, p))

    def h2(k):
        to = lax.rem(z + k, nz)
        return remote(head_slot, head_ring.at[z], h2_send.at[k], h2_recv.at[z], (to * 2 + core, col))

    def h2_from(k):
        source = lax.rem(z + k, nz)
        return remote(head_slot, head_ring.at[source], h2_send.at[k], h2_recv.at[source], (source * 2 + core, col))

    def head_rows(p):
        return head_all.at[:, pl.ds(pl.multiple_of(p * head_piece, 8), head_piece)]

    def h3(k):
        return remote(head_ring, head_rows(col), h3_send.at[k], h3_recv.at[col], (row, lax.rem(col + k, plane)))

    def h3_from(p):
        return remote(head_ring, head_rows(p), h3_send.at[0], h3_recv.at[p], (row, p))

    order = [(pair, d, c) for pair in range(2) for d, c in row_order]
    window = min(6, len(row_order) // 2)

    def issue(first, last):
        for i in range(first, min(last, len(order))):
            if window <= i < 2 * window:
                a2a(*order[i - window]).wait_send()
            a2a(*order[i]).start()

    @pl.when(jnp.logical_and(first_col, core == 1))
    def _():
        to_core0.start()

    issue(0, window)

    @pl.when(jnp.logical_and(first_col, head_core))
    def _():
        to_core0.wait_recv()
        head, head_cot = merge(turned[0, 0:slab, :], head_x[...], lane)
        head_own[...] = head
        here = pl.ds(pl.multiple_of(z * LANES, LANES), LANES)
        head_extra[...] = head * value_cot[:, here] + head_cot / values[:, here]
        loop(head_pieces, lambda p: h1(p).start(), 1)
        head_slot[...] = head[0:head_piece]

    @pl.when(jnp.logical_and(first_col, core == 1))
    def _():
        to_core0.wait_send()

    for pair in range(2):
        got[pair, row, 0:own_cols, :] = turned[pair, pl.ds(pl.multiple_of(row * own_cols, 8), own_cols), :]

    @pl.when(carries)
    def _():
        @pl.when(jnp.logical_not(first_col))
        def _():
            h1(col).wait_recv()
        loop(nz, lambda k: h2(k).start(), 1)
        head_ring[z] = head_slot[...]

    issue(window, 2 * window)

    @pl.when(carries)
    def _():
        loop(nz, lambda k: h2_from(k).wait_recv(), 1)
        loop(plane, lambda k: h3(k).start(), 1)
        head_all[:, pl.ds(pl.multiple_of(col * head_piece, 8), head_piece), :] = head_ring[...]

    issue(2 * window, len(order))

    def a2a_sent():
        for item in order[window:]:
            a2a(*item).wait_send()

    sent.append(a2a_sent)

    for j in range(nz):
        here = slice(j * LANES, (j + 1) * LANES)
        column[here, :] = jnp.broadcast_to(values[:, here] * values[:, here], (LANES, LANES)).T

    def gaps(j):
        here = pl.ds(pl.multiple_of(j * LANES, LANES), LANES)
        across_values = values[:, here]
        spacing = across_values * across_values - column[...]
        factor[:, here] = spacing / (spacing * spacing + BROADEN)

    loop(nz, gaps)

    def head_sent():
        @pl.when(jnp.logical_and(first_col, head_core))
        def _():
            loop(head_pieces, lambda p: h1(p).wait_send(), 1)

        @pl.when(carries)
        def _():
            loop(nz, lambda k: h2(k).wait_send(), 1)
            loop(plane, lambda k: h3(k).wait_send(), 1)

    sent.append(head_sent)

    def prepare(pair):
        lanes = lax.broadcasted_iota(jnp.int32, (LANES, LANES), 1)

        def take(j):
            first, second = merge(got[pair, 2 * j], got[pair, 2 * j + 1], lanes)
            here = pl.ds(pl.multiple_of(j * LANES, LANES), LANES)
            if pair == 1:
                p_own[:, here] = first
            for at, value in ((0, second), (LANES, first)):
                high, rest = split(value)
                rhs[pair, at:at + LANES, here] = high
                rhs[pair, 256 + at:256 + at + LANES, here] = high
                rhs[pair, 512 + at:512 + at + LANES, here] = rest
            for at, value in ((0, first.T), (LANES, -second.T)):
                high, rest = split(value)
                lhs[here, at:at + LANES] = high
                lhs[here, 256 + at:256 + at + LANES] = rest
                lhs[here, 512 + at:512 + at + LANES] = high

        a2a_from(pair, other).wait_recv()
        take(z)

        def arrive(i):
            d = nz // 2 + ((i + 1) // 2) * (1 - 2 * (i % 2))
            j = lax.rem(z + nz - d, nz)
            a2a_from(pair, 2 * j).wait_recv()
            a2a_from(pair, 2 * j + 1).wait_recv()
            take(j)

        loop(nz - 1, arrive)

    def through(stacked, count, high, rest, dot):
        both = dot(stacked, high)
        return both[:count] + both[count:] + dot(stacked[:count], rest)

    def low_rank(which, pair, at):
        value = through(heads[which], slab, rhs[pair, at:at + LANES, :], rhs[pair, 512 + at:512 + at + LANES, :], dot_nt)
        high, rest = split(value)
        low[0:slab, :] = high
        low[slab:, :] = rest
        return value

    def columns(pair, j):
        here = pl.ds(pl.multiple_of(j * block, block), block)
        right = rhs[pair, :, here]
        for i in range(keep // 256):
            there = slice(i * 256, (i + 1) * 256)
            high, rest = split(factor[there, here] * dot_nn(lhs[there, :], right))
            sym_high[there, :] = high
            sym_rest[there, :] = rest
        total = through(heads[pair], slab, sym_high[...], sym_rest[...], dot_nn)
        at = LANES * pair
        outer = through(low[...], slab, right[at:at + LANES], right[512 + at:512 + at + LANES], dot_nn)
        if pair == 0:
            w_acc[:, here] = total * values[:, here] - outer / values[:, here]
            return
        total = w_acc[:, here] + total - outer
        for t in range(block // LANES):
            for h in range(2):
                for g in range(groups):
                    start = h * half + g * piece
                    w_part[h, (j * (block // LANES) + t) * groups + g] = total[start:start + piece, t * LANES:(t + 1) * LANES]

    prepare(0)

    to_core1 = remote(head_all, head_all, core_send.at[1], core_recv.at[1], (other, col))

    @pl.when(head_core)
    def _():
        def arrived(p):
            @pl.when(p != col)
            def _():
                h3_from(p).wait_recv()
        loop(head_pieces, arrived)
        to_core1.start()

    @pl.when(core == 1)
    def _():
        to_core1.wait_recv()

    def head_core_sent():
        @pl.when(head_core)
        def _():
            to_core1.wait_send()

    sent.append(head_core_sent)

    def head_parts(j):
        here = pl.ds(pl.multiple_of(j * LANES, LANES), LANES)
        head = head_all[j]
        for which, value in enumerate((head, head * values[:, here], head / values[:, here])):
            high, rest = split(value)
            heads[which, 0:slab, here] = high
            heads[which, slab:, here] = rest

    loop(nz, head_parts)
    low_rank(0, 0, LANES)
    loop(keep // block, functools.partial(columns, 0))

    @pl.when(jnp.logical_and(first_col, head_core))
    def _():
        here = pl.ds(pl.multiple_of(z * LANES, LANES), LANES)
        w_acc[:, here] = w_acc[:, here] + head_extra[...]

    prepare(1)
    third[...] = low_rank(2, 1, 0)
    p_swap = remote(p_own, p_other, core_send.at[2], core_recv.at[2], (other, col))
    third_swap = remote(third.at[pl.ds(pl.multiple_of((1 - core) * half, 8), half)], third_other,
                        core_send.at[3], core_recv.at[3], (other, col))
    p_swap.start()
    third_swap.start()
    sent.extend((p_swap.wait_send, third_swap.wait_send))

    per = groups * block // LANES

    def w_swap(j):
        part = pl.ds(j * per, per)
        return remote(w_part.at[1 - core, part], w_other.at[part],
                      core_send.at[4 + j], core_recv.at[4 + j], (other, col))

    def rs(p):
        return remote(rs_src.at[p], rs_buf.at[me], rs_send.at[p], rs_recv.at[me], plane_device(p))

    def rs_from(source):
        return remote(rs_src.at[source], rs_buf.at[source], rs_send.at[source], rs_recv.at[source],
                      plane_device(source))

    def scatter(j):
        w_swap(j).wait_recv()
        part = pl.ds(j * per, per)
        rs_src[part] = w_part[core, part] + w_other[part]

        def one(i):
            p = j * per + lax.rem(me + i, per)

            @pl.when(p != me)
            def _():
                rs(p).start()
        loop(per, one)

    def rs_sent():
        def one(p):
            @pl.when(p != me)
            def _():
                rs(p).wait_send()
        loop(plane, one)

    for j in range(keep // block):
        columns(1, j)
        w_swap(j).start()
        sent.append(w_swap(j).wait_send)
        if j:
            scatter(j - 1)
    scatter(keep // block - 1)
    sent.append(rs_sent)
    rs_buf[me] = rs_src[me]
    loop(plane, lambda k: rs_from(lax.rem(me + k, plane)).wait_recv(), 1)
    ar_src[...] = jnp.sum(rs_buf[...], axis=0)

    def ar(k):
        to = lax.rem(across + k, nz)
        return remote(ar_src, ar_buf.at[across], ar_send.at[k], ar_recv.at[across], line_device(to))

    def ar_from(k):
        source = lax.rem(across + k, nz)
        return remote(ar_src, ar_buf.at[source], ar_send.at[k], ar_recv.at[source], line_device(source))

    for d in line_order:
        ar(d).start()
    sent.append(lambda: loop(nz, lambda k: ar(k).wait_send(), 1))
    ar_buf[across] = ar_src[...]
    loop(nz, lambda k: ar_from(k).wait_recv(), 1)
    ag_src[...] = jnp.sum(ar_buf[...], axis=0)

    def ag(to):
        return remote(ag_src, w_full.at[me], ag_send.at[to], ag_recv.at[me], plane_device(to))

    def ag_from(k):
        source = lax.rem(me + k, plane)
        return remote(ag_src, w_full.at[source], ag_send.at[source], ag_recv.at[source], plane_device(source))

    for dx, dt in plane_order:
        ag(around(dx, dt)).start()
    sent.append(lambda: loop(plane, lambda k: ag(lax.rem(me + k, plane)).wait_send(), 1))
    w_full[me] = ag_src[...]
    p_swap.wait_recv()
    third_swap.wait_recv()
    loop(plane, lambda k: ag_from(k).wait_recv(), 1)

    mine = jnp.zeros((half, LANES), F32)
    theirs = jnp.zeros((half, LANES), F32)
    for j in range(nz):
        here = slice(j * LANES, (j + 1) * LANES)
        high, rest = split(jnp.concatenate([w_full[j * groups + g] for g in range(groups)], axis=0))
        stacked = jnp.concatenate([high, rest], axis=0)
        mine = mine + through(stacked, half, rhs[1, LANES:256, here], rhs[1, 640:768, here], dot_nt)
        theirs = theirs + through(stacked, half, *split(p_other[:, here]), dot_nt)
    mine = mine + third[pl.ds(pl.multiple_of(core * half, 8), half), :]
    theirs = theirs + third_other[...]
    for i in range(nz):
        for at, value in ((core, mine), (1 - core, theirs)):
            out_src[i, at] = jnp.pad(value[i * out_rows:(i + 1) * out_rows], ((0, 16 - out_rows), (0, 0)))

    def send_out(i):
        to = core * nz + i
        return remote(out_src.at[i], out_buf.at[z], o_send.at[i], o_recv.at[z], (to, col))

    def out_from(i):
        source = 2 * i + row // nz
        return remote(out_src.at[i], out_buf.at[i], o_send.at[i], o_recv.at[i], (source, col))

    def each_out(step):
        def run(i):
            @pl.when(core * nz + i != row)
            def _():
                step(send_out(i))
        loop(nz, run)

    each_out(lambda copy: copy.start())

    @pl.when(core == row // nz)
    def _():
        out_buf[z] = out_src[lax.rem(row, nz)]

    def out_arrived(i):
        @pl.when(2 * i + row // nz != row)
        def _():
            out_from(i).wait_recv()
    loop(nz, out_arrived)
    for i in range(nz):
        for c in range(2):
            start = (2 * i + c) * own_cols
            out[:, start:start + own_cols] = out_buf[i, c, 0:out_rows, 0:own_cols]

    each_out(lambda copy: copy.wait_send())
    settle()


def body(nx, ny, nz, slab, scale, left_vecs, left_cot, right_vecs, right_cot, values, value_cot):
    rows_n, plane, keep, width = 2 * nz, nx * ny, values.shape[0], left_vecs.shape[1]
    own_cols, half = width // rows_n, slab // 2
    piece = half // (plane // nz)
    head_piece = -(-(-(-slab // plane)) // 8) * 8
    pieces = (plane, piece, LANES)
    dma = pltpu.SemaphoreType.DMA
    scratch = [
        pltpu.VMEM((2, LANES, width), F32),
        pltpu.VMEM((2, width, LANES), F32),
        pltpu.VMEM((2, rows_n, LANES, LANES), F32),
        pltpu.VMEM((keep, 768), BF16),
        pltpu.VMEM((2, 768, keep), BF16),
        pltpu.VMEM((LANES, keep), F32),
        pltpu.VMEM((LANES, keep), F32),
        pltpu.VMEM((keep, LANES), F32),
        pltpu.VMEM((keep, keep), F32),
        pltpu.VMEM((3, 2 * slab, keep), BF16),
        pltpu.VMEM((slab, LANES), F32),
        pltpu.VMEM((slab, LANES), F32),
        pltpu.VMEM((slab, LANES), F32),
        pltpu.VMEM((head_piece, LANES), F32),
        pltpu.VMEM((nz, head_piece, LANES), F32),
        pltpu.VMEM((nz, slab, LANES), F32),
        pltpu.VMEM((slab, keep), F32),
        pltpu.VMEM((2,) + pieces, F32),
        pltpu.VMEM(pieces, F32),
        pltpu.VMEM(pieces, F32),
        pltpu.VMEM(pieces, F32),
        pltpu.VMEM((piece, LANES), F32),
        pltpu.VMEM((nz, piece, LANES), F32),
        pltpu.VMEM((piece, LANES), F32),
        pltpu.VMEM(pieces, F32),
        pltpu.VMEM((keep, keep // 2), BF16),
        pltpu.VMEM((keep, keep // 2), BF16),
        pltpu.VMEM((2 * slab, LANES), BF16),
        pltpu.VMEM((slab, LANES), F32),
        pltpu.VMEM((half, LANES), F32),
        pltpu.VMEM((nz, 2, 16, LANES), F32),
        pltpu.VMEM((nz, 2, 16, LANES), F32),
        dma((4,)), dma((2, rows_n)), dma((2, rows_n)), dma((4 + keep // LANES,)), dma((4 + keep // LANES,)),
        dma((plane,)), dma((1,)), dma((nz,)), dma((nz,)), dma((plane,)), dma((plane,)),
        dma((plane,)), dma((plane,)), dma((nz,)), dma((nz,)), dma((plane,)), dma((plane,)),
        dma((nz,)), dma((nz,)),
    ]
    vmem, anywhere = pl.BlockSpec(memory_space=pltpu.VMEM), pl.BlockSpec(memory_space=pl.ANY)
    return pl.pallas_call(
        functools.partial(kernel, (nx, ny, nz, piece, head_piece, slab, own_cols)),
        out_shape=jax.ShapeDtypeStruct((slab // rows_n, width), F32),
        in_specs=[anywhere] * 4 + [vmem] * 2,
        out_specs=vmem,
        scratch_shapes=scratch,
        compiler_params=pltpu.CompilerParams(
            collective_id=0, has_side_effects=True, vmem_limit_bytes=56 * 1024 * 1024),
        cost_estimate=pl.CostEstimate(flops=12 * 2**30, bytes_accessed=2 * 2**20, transcendentals=0),
    )(left_vecs, left_cot, right_vecs, right_cot, values[None, :], value_cot[None, :]) * scale


def build(mesh, nx, ny, nz, slab, scale):
    panel = P("row", "col")
    return jax.shard_map(
        functools.partial(body, nx, ny, nz, slab, scale), mesh=mesh,
        in_specs=(panel, panel, panel, panel, P(), P()), out_specs=panel, check_vma=False)


def solution(mesh):
    return build(mesh, 4, 8, 8, SLAB, ORDER / math.sqrt(KEEP))
```

```python
import functools
import math

import jax
import jax.numpy as jnp
from jax import lax
from jax.experimental import pallas as pl
from jax.experimental.pallas import tpu as pltpu
from jax.sharding import PartitionSpec as P

ORDER = 53248
KEEP = 1024
SLAB = 192
BROADEN = 0.0001
LANES = 128
F32 = jnp.float32
BF16 = jnp.bfloat16


def split(value):
    high = value.astype(BF16)
    return high, (value - high.astype(F32)).astype(BF16)


def dot_nn(left, right):
    return lax.dot_general(left, right, (((1,), (0,)), ((), ())), preferred_element_type=F32)


def dot_nt(left, right):
    return lax.dot_general(left, right, (((1,), (1,)), ((), ())), preferred_element_type=F32)


def kernel(geo, *refs):
    nx, ny, nz, piece, head_piece, slab, own_cols = geo
    rows_n = 2 * nz
    plane = nx * ny
    keep = nz * LANES
    half = slab // 2
    out_rows = slab // rows_n
    width = own_cols * rows_n
    head_pieces = slab // head_piece
    groups = half // piece
    block = keep // 2
    (a_in, b_in, p_in, q_in, values, value_cot, out_buf,
     panels, turned, got, lhs, rhs, p_own, p_other, column, factor,
     heads, head_own, head_x, head_extra, head_slot, head_ring, head_all,
     w_acc, w_part, w_other, rs_src, rs_buf, ar_src, ar_buf, ag_src, w_full,
     sym_high, sym_rest, low, third, third_other, last_left, last_high, last_rest, out_src,
     load_sem, a2a_send, a2a_recv, core_send, core_recv, head_send, head_recv, sum_send, sum_recv, own_sem) = refs

    row = lax.axis_index("row")
    col = lax.axis_index("col")
    z, core = row // 2, row % 2
    x, y = col // ny, col % ny
    other = z * 2 + 1 - core
    along = (1 - core) * y + core * z
    across = (1 - core) * z + core * y
    me = x * ny + along

    def plane_device(index):
        px, pt = index // ny, index % ny
        py = (1 - core) * pt + core * y
        pz = (1 - core) * z + core * pt
        return (pz * 2 + core, px * ny + py)

    def line_device(index):
        py = (1 - core) * y + core * index
        pz = (1 - core) * index + core * z
        return (pz * 2 + core, x * ny + py)

    def remote(src, dst, send, recv, device):
        return pltpu.make_async_remote_copy(
            src_ref=src, dst_ref=dst, send_sem=send, recv_sem=recv,
            device_id=device, device_id_type=pl.DeviceIdType.MESH)

    def loop(count, step, first=0):
        def run(i, carry):
            step(i)
            return carry
        lax.fori_loop(first, count, run, 0)

    line_order = sorted(range(1, nz), key=lambda d: -min(d, nz - d))
    plane_order = sorted(
        ((dx, dt) for dx in range(nx) for dt in range(ny) if dx or dt),
        key=lambda at: -min(at[0], nx - at[0]) - min(at[1], ny - at[1]))
    row_order = [(0, 0)] + [(d, c) for d in line_order for c in range(2)]

    def around(dx, dt):
        return lax.rem(x + dx, nx) * ny + lax.rem(along + dt, ny)

    def row_target(d, c):
        return lax.rem(z + d, nz) * 2 + c if d else other

    sent = []

    def settle():
        for step in sent:
            step()

    barrier = pltpu.get_barrier_semaphore()

    def greet(device):
        pl.semaphore_signal(barrier, inc=1, device_id=device, device_id_type=pl.DeviceIdType.MESH)

    for dx, dt in plane_order:
        greet(plane_device(around(dx, dt)))
    for d in line_order:
        greet(line_device(lax.rem(across + d, nz)))
    for d, c in row_order:
        greet((row_target(d, c), col))

    for i, source in enumerate((a_in, b_in, p_in, q_in)):
        pltpu.make_async_copy(source, panels.at[i // 2, pl.ds(64 * (i % 2), 64)], load_sem.at[i // 2]).start()

    def turn(pair):
        pltpu.make_async_copy(panels.at[pair], panels.at[pair], load_sem.at[pair]).wait()
        for tile in range(width // LANES):
            turned[pair, tile * LANES:(tile + 1) * LANES, :] = panels[pair, :, tile * LANES:(tile + 1) * LANES].T

    turn(0)
    pl.semaphore_wait(barrier, rows_n - 1 + plane - 1 + nz - 1)

    def arrival(pair, chip):
        return a2a_recv.at[0 if pair == 0 else 1 + chip]

    def a2a(pair, d, c, send):
        to = row_target(d, c)
        return remote(
            turned.at[pair, pl.ds(pl.multiple_of(to * own_cols, 8), own_cols)],
            got.at[pair, row, pl.ds(0, own_cols)],
            a2a_send.at[send], arrival(pair, z), (to, col))

    def landed(ref, semaphore):
        remote(ref, ref, core_send.at[0], semaphore, (other, col)).wait_recv()

    def left(ref, semaphore):
        remote(ref, ref, semaphore, core_recv.at[0], (other, col)).wait_send()

    first_col = col == 0
    head_core = core == 0
    carries = jnp.logical_and(head_core, col < head_pieces)
    lane = lax.broadcasted_iota(jnp.int32, (slab, LANES), 1)

    def merge(left, right, lanes):
        return (jnp.where(lanes < 64, left, pltpu.roll(right, 64, 1)),
                jnp.where(lanes < 64, pltpu.roll(left, 64, 1), right))

    to_core0 = remote(turned.at[0, pl.ds(0, slab)], head_x, core_send.at[0], core_recv.at[0], (other, col))

    def h1(p):
        return remote(head_own.at[pl.ds(pl.multiple_of(p * head_piece, 8), head_piece)], head_slot,
                      head_send.at[0], head_recv.at[0], (row, p))

    def h2(d):
        return remote(head_slot, head_ring.at[z], head_send.at[1], head_recv.at[1],
                      (lax.rem(z + d, nz) * 2 + core, col))

    def h3(k):
        return remote(head_ring, head_all.at[:, pl.ds(pl.multiple_of(col * head_piece, 8), head_piece)],
                      head_send.at[2], head_recv.at[2], (row, lax.rem(col + k, plane)))

    order = [(pair, d, c) for pair in range(2) for d, c in row_order]
    window = min(6, len(row_order) // 2)

    def issue(first, last):
        for i in range(first, min(last, len(order))):
            if window <= i < 2 * window:
                left(turned.at[0, pl.ds(0, own_cols)], a2a_send.at[i - window])
            a2a(*order[i], i if i < window else window + order[i][0]).start()

    @pl.when(jnp.logical_and(first_col, core == 1))
    def _():
        to_core0.start()

    issue(0, window)

    @pl.when(jnp.logical_and(first_col, head_core))
    def _():
        to_core0.wait_recv()
        head, head_cot = merge(turned[0, 0:slab, :], head_x[...], lane)
        head_own[...] = head
        here = pl.ds(pl.multiple_of(z * LANES, LANES), LANES)
        head_extra[...] = head * value_cot[:, here] + head_cot / values[:, here]
        loop(head_pieces, lambda p: h1(p).start(), 1)
        head_slot[...] = head[0:head_piece]

    @pl.when(jnp.logical_and(first_col, core == 1))
    def _():
        to_core0.wait_send()

    turn(1)
    got[:, :, own_cols:, :] = jnp.zeros((2, rows_n, LANES - own_cols, LANES), F32)
    for pair in range(2):
        got[pair, row, 0:own_cols, :] = turned[pair, pl.ds(pl.multiple_of(row * own_cols, 8), own_cols), :]

    @pl.when(carries)
    def _():
        @pl.when(jnp.logical_not(first_col))
        def _():
            landed(head_slot, head_recv.at[0])
        for d in line_order:
            h2(d).start()
        head_ring[z] = head_slot[...]

    issue(window, 2 * window)

    @pl.when(carries)
    def _():
        landed(head_ring.at[pl.ds(0, nz - 1)], head_recv.at[1])
        loop(plane, lambda k: h3(k).start(), 1)
        head_all[:, pl.ds(pl.multiple_of(col * head_piece, 8), head_piece), :] = head_ring[...]

    issue(2 * window, len(order))

    def a2a_sent():
        left(turned.at[0, pl.ds(0, (len(row_order) - window) * own_cols)], a2a_send.at[window])
        left(turned.at[1, pl.ds(0, len(row_order) * own_cols)], a2a_send.at[window + 1])

    sent.append(a2a_sent)

    for j in range(nz):
        here = slice(j * LANES, (j + 1) * LANES)
        column[here, :] = jnp.broadcast_to(values[:, here] * values[:, here], (LANES, LANES)).T

    def gaps(j):
        here = pl.ds(pl.multiple_of(j * LANES, LANES), LANES)
        across_values = values[:, here]
        spacing = across_values * across_values - column[...]
        factor[:, here] = spacing / (spacing * spacing + BROADEN)

    loop(nz, gaps)

    def head_sent():
        @pl.when(jnp.logical_and(first_col, head_core))
        def _():
            left(head_own.at[pl.ds(0, slab - head_piece)], head_send.at[0])

        @pl.when(carries)
        def _():
            left(head_ring.at[pl.ds(0, nz - 1)], head_send.at[1])
            left(factor.at[pl.ds(0, (plane - 1) * head_piece)], head_send.at[2])

    sent.append(head_sent)

    def through(stacked, count, high, rest, dot):
        both = dot(stacked, high)
        return both[:count] + both[count:] + dot(stacked[:count], rest)

    def prepare(pair):
        lanes = lax.broadcasted_iota(jnp.int32, (LANES, LANES), 1)

        def take(j):
            first, second = merge(got[pair, 2 * j], got[pair, 2 * j + 1], lanes)
            here = pl.ds(pl.multiple_of(j * LANES, LANES), LANES)
            if pair == 1:
                p_own[:, here] = first
            for at, value in ((0, second), (LANES, first)):
                high, rest = split(value)
                rhs[pair, at:at + LANES, here] = high
                rhs[pair, 256 + at:256 + at + LANES, here] = high
                rhs[pair, 512 + at:512 + at + LANES, here] = rest
                if pair == 1 and at == 0:
                    third[...] = third[...] + through(heads[2, :, here], slab, high, rest, dot_nt)
            for at, value in ((0, first.T), (LANES, -second.T)):
                high, rest = split(value)
                lhs[here, at:at + LANES] = high
                lhs[here, 256 + at:256 + at + LANES] = rest
                lhs[here, 512 + at:512 + at + LANES] = high

        def arrive(i):
            d = nz // 2 + ((i + 1) // 2) * (1 - 2 * (i % 2))
            j = lax.rem(z + nz - d, nz)
            if pair == 1:
                landed(got.at[pair, pl.ds(2 * j, 2), pl.ds(0, own_cols)], arrival(pair, j))
            take(j)

        if pair == 0:
            landed(got.at[pair, pl.ds(0, rows_n - 1), pl.ds(0, own_cols)], arrival(pair, z))
        else:
            landed(got.at[pair, 0, pl.ds(0, own_cols)], arrival(pair, z))
        take(z)
        loop(nz - 1, arrive)

    def set_low(value):
        high, rest = split(value)
        low[0:slab, :] = high
        low[slab:, :] = rest

    def columns(pair, j):
        here = pl.ds(pl.multiple_of(j * block, block), block)
        right = rhs[pair, :, here]
        for i in range(keep // 256):
            there = slice(i * 256, (i + 1) * 256)
            high, rest = split(factor[there, here] * dot_nn(lhs[there, :], right))
            sym_high[there, :] = high
            sym_rest[there, :] = rest
        total = through(heads[pair], slab, sym_high[...], sym_rest[...], dot_nn)
        at = LANES * pair
        outer = through(low[...], slab, right[at:at + LANES], right[512 + at:512 + at + LANES], dot_nn)
        if pair == 0:
            w_acc[:, here] = total * values[:, here] - outer / values[:, here]
            return
        total = w_acc[:, here] + total - outer
        for t in range(block // LANES):
            for h in range(2):
                for g in range(groups):
                    start = h * half + g * piece
                    w_part[h, (j * (block // LANES) + t) * groups + g] = total[start:start + piece, t * LANES:(t + 1) * LANES]

    prepare(0)

    to_core1 = remote(head_all, head_all, core_send.at[1], core_recv.at[1], (other, col))

    @pl.when(head_core)
    def _():
        @pl.when(col < head_pieces)
        def _():
            landed(head_all.at[:, pl.ds(0, slab - head_piece)], head_recv.at[2])

        @pl.when(col >= head_pieces)
        def _():
            landed(head_all, head_recv.at[2])
        to_core1.start()

    @pl.when(core == 1)
    def _():
        to_core1.wait_recv()

    def head_core_sent():
        @pl.when(head_core)
        def _():
            to_core1.wait_send()

    sent.append(head_core_sent)

    def head_parts(j):
        here = pl.ds(pl.multiple_of(j * LANES, LANES), LANES)
        head = head_all[j]
        for which, value in enumerate((head, head * values[:, here], head / values[:, here])):
            high, rest = split(value)
            heads[which, 0:slab, here] = high
            heads[which, slab:, here] = rest

    loop(nz, head_parts)
    set_low(through(heads[0], slab, rhs[0, LANES:256, :], rhs[0, 640:768, :], dot_nt))
    loop(keep // block, functools.partial(columns, 0))

    @pl.when(jnp.logical_and(first_col, head_core))
    def _():
        here = pl.ds(pl.multiple_of(z * LANES, LANES), LANES)
        w_acc[:, here] = w_acc[:, here] + head_extra[...]

    third[...] = jnp.zeros((slab, LANES), F32)
    prepare(1)
    set_low(third[...])
    p_swap = remote(p_own, p_other, core_send.at[2], core_recv.at[2], (other, col))
    third_swap = remote(third.at[pl.ds(pl.multiple_of((1 - core) * half, 8), half)], third_other,
                        core_send.at[3], core_recv.at[3], (other, col))
    p_swap.start()
    third_swap.start()
    sent.extend((p_swap.wait_send, third_swap.wait_send))

    per = groups * block // LANES

    def w_swap(j):
        part = pl.ds(j * per, per)
        return remote(w_part.at[1 - core, part], w_other.at[part],
                      core_send.at[4 + j], core_recv.at[4 + j], (other, col))

    mine_now = (lax.rem(along, 2) * (nz // 2) + along // 2) * groups + x

    def owner(q):
        zb, g = q // groups, q % groups
        return g * ny + 2 * (zb % (nz // 2)) + zb // (nz // 2)

    def rs(q):
        return remote(rs_src.at[q], rs_buf.at[me], sum_send.at[0], sum_recv.at[0], plane_device(owner(q)))

    def scatter(j):
        w_swap(j).wait_recv()
        part = pl.ds(j * per, per)
        rs_src[part] = w_part[core, part] + w_other[part]

        def one(i):
            q = j * per + lax.rem(me + i, per)

            @pl.when(q != mine_now)
            def _():
                rs(q).start()
        loop(per, one)

    for j in range(keep // block):
        columns(1, j)
        w_swap(j).start()
        sent.append(w_swap(j).wait_send)
        if j:
            scatter(j - 1)
    scatter(keep // block - 1)
    sent.append(lambda: left(rs_buf.at[pl.ds(0, plane - 1)], sum_send.at[0]))
    rs_buf[me] = rs_src[mine_now]
    landed(rs_buf.at[pl.ds(0, plane - 1)], sum_recv.at[0])
    ar_src[...] = jnp.sum(rs_buf[...], axis=0)

    for d in line_order:
        remote(ar_src, ar_buf.at[across], sum_send.at[1], sum_recv.at[1],
               line_device(lax.rem(across + d, nz))).start()
    sent.append(lambda: left(ar_buf.at[pl.ds(0, nz - 1)], sum_send.at[1]))
    ar_buf[across] = ar_src[...]
    landed(ar_buf.at[pl.ds(0, nz - 1)], sum_recv.at[1])
    ag_src[...] = jnp.sum(ar_buf[...], axis=0)

    for dx, dt in plane_order:
        remote(ag_src, w_full.at[me], sum_send.at[2], sum_recv.at[2], plane_device(around(dx, dt))).start()
    sent.append(lambda: left(w_full.at[pl.ds(0, plane - 1)], sum_send.at[2]))
    w_full[me] = ag_src[...]
    p_swap.wait_recv()
    third_swap.wait_recv()
    last_high[0:LANES, :] = rhs[1, LANES:256, :]
    last_rest[0:LANES, :] = rhs[1, 640:768, :]
    high, rest = split(p_other[...])
    last_high[LANES:, :] = high
    last_rest[LANES:, :] = rest
    landed(w_full.at[pl.ds(0, plane - 1)], sum_recv.at[2])

    for zb in range(nz):
        here = slice(zb * LANES, (zb + 1) * LANES)
        t = 2 * (zb % (nz // 2)) + zb // (nz // 2)
        high, rest = split(jnp.concatenate([w_full[g * ny + t] for g in range(groups)], axis=0))
        last_left[0:half, here] = high
        last_left[half:, here] = rest
    product = through(last_left[...], half, last_high[...], last_rest[...], dot_nt)
    mine = product[:, :LANES] + third[pl.ds(pl.multiple_of(core * half, 8), half), :]
    theirs = product[:, LANES:] + third_other[...]
    for i in range(nz):
        for at, value in ((core, mine), (1 - core, theirs)):
            out_src[i, at] = value[i * out_rows:(i + 1) * out_rows]

    def send_out(i):
        return remote(out_src.at[i], out_buf.at[z], sum_send.at[3], sum_recv.at[3], (core * nz + i, col))

    for d in range(nz):
        i = lax.rem(z + d + nz // 2, nz)

        @pl.when(core * nz + i != row)
        def _():
            send_out(i).start()

    keeps = core == row // nz
    own_out = pltpu.make_async_copy(out_src.at[lax.rem(row, nz)], out_buf.at[z], own_sem.at[0])

    @pl.when(keeps)
    def _():
        own_out.start()
        landed(out_buf.at[pl.ds(0, nz - 1)], sum_recv.at[3])
        left(out_src.at[pl.ds(0, nz - 1)], sum_send.at[3])
        own_out.wait()

    @pl.when(jnp.logical_not(keeps))
    def _():
        landed(out_buf, sum_recv.at[3])
        left(out_src, sum_send.at[3])

    settle()


def lay_out(own_cols, scale, blocks, out):
    for i in range(blocks.shape[0]):
        for c in range(2):
            start = (2 * i + c) * own_cols
            out[:, start:start + own_cols] = blocks[i, c, :, 0:own_cols] * scale


def body(nx, ny, nz, slab, scale, left_vecs, left_cot, right_vecs, right_cot, values, value_cot):
    rows_n, plane, keep, width = 2 * nz, nx * ny, values.shape[0], left_vecs.shape[1]
    own_cols, half = width // rows_n, slab // 2
    piece = half // (plane // nz)
    head_piece = -(-(-(-slab // plane)) // 8) * 8
    pieces = (plane, piece, LANES)
    dma = pltpu.SemaphoreType.DMA
    scratch = [
        pltpu.VMEM((2, LANES, width), F32),
        pltpu.VMEM((2, width, LANES), F32),
        pltpu.VMEM((2, rows_n, LANES, LANES), F32),
        pltpu.VMEM((keep, 768), BF16),
        pltpu.VMEM((2, 768, keep), BF16),
        pltpu.VMEM((LANES, keep), F32),
        pltpu.VMEM((LANES, keep), F32),
        pltpu.VMEM((keep, LANES), F32),
        pltpu.VMEM((keep, keep), F32),
        pltpu.VMEM((3, 2 * slab, keep), BF16),
        pltpu.VMEM((slab, LANES), F32),
        pltpu.VMEM((slab, LANES), F32),
        pltpu.VMEM((slab, LANES), F32),
        pltpu.VMEM((head_piece, LANES), F32),
        pltpu.VMEM((nz, head_piece, LANES), F32),
        pltpu.VMEM((nz, slab, LANES), F32),
        pltpu.VMEM((slab, keep), F32),
        pltpu.VMEM((2,) + pieces, F32),
        pltpu.VMEM(pieces, F32),
        pltpu.VMEM(pieces, F32),
        pltpu.VMEM(pieces, F32),
        pltpu.VMEM((piece, LANES), F32),
        pltpu.VMEM((nz, piece, LANES), F32),
        pltpu.VMEM((piece, LANES), F32),
        pltpu.VMEM(pieces, F32),
        pltpu.VMEM((keep, keep // 2), BF16),
        pltpu.VMEM((keep, keep // 2), BF16),
        pltpu.VMEM((2 * slab, LANES), BF16),
        pltpu.VMEM((slab, LANES), F32),
        pltpu.VMEM((half, LANES), F32),
        pltpu.VMEM((2 * half, keep), BF16),
        pltpu.VMEM((2 * LANES, keep), BF16),
        pltpu.VMEM((2 * LANES, keep), BF16),
        pltpu.VMEM((nz, 2, slab // rows_n, LANES), F32),
        dma((2,)), dma((8,)), dma((1 + nz,)), dma((6,)), dma((6,)), dma((3,)), dma((3,)),
        dma((4,)), dma((4,)), dma((1,)),
    ]
    vmem, anywhere = pl.BlockSpec(memory_space=pltpu.VMEM), pl.BlockSpec(memory_space=pl.ANY)
    blocks = pl.pallas_call(
        functools.partial(kernel, (nx, ny, nz, piece, head_piece, slab, own_cols)),
        out_shape=jax.ShapeDtypeStruct((nz, 2, slab // rows_n, LANES), F32),
        in_specs=[anywhere] * 4 + [vmem] * 2,
        out_specs=anywhere,
        scratch_shapes=scratch,
        compiler_params=pltpu.CompilerParams(
            collective_id=0, has_side_effects=True, vmem_limit_bytes=56 * 1024 * 1024),
        cost_estimate=pl.CostEstimate(flops=12 * 2**30, bytes_accessed=2 * 2**20, transcendentals=0),
    )(left_vecs, left_cot, right_vecs, right_cot, values[None, :], value_cot[None, :])
    return pl.pallas_call(
        functools.partial(lay_out, own_cols, scale),
        out_shape=jax.ShapeDtypeStruct((slab // rows_n, width), F32),
        in_specs=[vmem], out_specs=vmem,
    )(blocks)


def build(mesh, nx, ny, nz, slab, scale):
    panel = P("row", "col")
    return jax.shard_map(
        functools.partial(body, nx, ny, nz, slab, scale), mesh=mesh,
        in_specs=(panel, panel, panel, panel, P(), P()), out_specs=panel, check_vma=False)


def solution(mesh):
    return build(mesh, 4, 8, 8, SLAB, ORDER / math.sqrt(KEEP))
```

```python
import functools
import math

import jax
import jax.numpy as jnp
from jax import lax
from jax.experimental import pallas as pl
from jax.experimental.pallas import tpu as pltpu
from jax.sharding import PartitionSpec as P

ORDER = 53248
KEEP = 1024
SLAB = 192
BROADEN = 0.0001
LANES = 128
F32 = jnp.float32
BF16 = jnp.bfloat16


def split(value):
    high = value.astype(BF16)
    return high, (value - high.astype(F32)).astype(BF16)


def dot_nn(left, right):
    return lax.dot_general(left, right, (((1,), (0,)), ((), ())), preferred_element_type=F32)


def dot_nt(left, right):
    return lax.dot_general(left, right, (((1,), (1,)), ((), ())), preferred_element_type=F32)


def kernel(geo, *refs):
    nx, ny, nz, piece, head_piece, slab, own_cols = geo
    rows_n = 2 * nz
    plane = nx * ny
    keep = nz * LANES
    half = slab // 2
    out_rows = slab // rows_n
    width = own_cols * rows_n
    head_pieces = slab // head_piece
    groups = half // piece
    block = keep // 2
    (a_in, b_in, p_in, q_in, values, value_cot, out_buf,
     panels, turned, got, lhs, rhs, p_own, p_other, column, factor,
     heads, head_own, head_x, head_extra, head_slot, head_ring, head_all,
     w_acc, w_part, w_other, rs_src, rs_buf, ar_src, ar_buf, ag_src, w_full,
     sym_high, sym_rest, low, third, third_other, last_left, last_high, last_rest, out_src,
     load_sem, a2a_send, a2a_recv, core_send, core_recv, head_send, head_recv, sum_send, sum_recv, own_sem) = refs

    row = lax.axis_index("row")
    col = lax.axis_index("col")
    z, core = row // 2, row % 2
    x, y = col // ny, col % ny
    other = z * 2 + 1 - core
    along = (1 - core) * y + core * z
    across = (1 - core) * z + core * y
    me = x * ny + along

    def plane_device(index):
        px, pt = index // ny, index % ny
        py = (1 - core) * pt + core * y
        pz = (1 - core) * z + core * pt
        return (pz * 2 + core, px * ny + py)

    def line_device(index):
        py = (1 - core) * y + core * index
        pz = (1 - core) * index + core * z
        return (pz * 2 + core, x * ny + py)

    def remote(src, dst, send, recv, device):
        return pltpu.make_async_remote_copy(
            src_ref=src, dst_ref=dst, send_sem=send, recv_sem=recv,
            device_id=device, device_id_type=pl.DeviceIdType.MESH)

    def loop(count, step, first=0):
        def run(i, carry):
            step(i)
            return carry
        lax.fori_loop(first, count, run, 0)

    line_order = sorted(range(1, nz), key=lambda d: -min(d, nz - d))
    plane_order = sorted(
        ((dx, dt) for dx in range(nx) for dt in range(ny) if dx or dt),
        key=lambda at: -min(at[0], nx - at[0]) - min(at[1], ny - at[1]))
    row_order = [(0, 0)] + [(d, c) for d in line_order for c in range(2)]

    def around(dx, dt):
        return lax.rem(x + dx, nx) * ny + lax.rem(along + dt, ny)

    def row_target(d, c):
        return lax.rem(z + d, nz) * 2 + c if d else other

    sent = []

    def settle():
        for step in sent:
            step()

    barrier = pltpu.get_barrier_semaphore()

    def greet(device):
        pl.semaphore_signal(barrier, inc=1, device_id=device, device_id_type=pl.DeviceIdType.MESH)

    for i, source in enumerate((a_in, b_in, p_in, q_in)):
        pltpu.make_async_copy(source, panels.at[i // 2, pl.ds(64 * (i % 2), 64)], load_sem.at[i // 2]).start()

    for dx, dt in plane_order:
        greet(plane_device(around(dx, dt)))
    for d in line_order:
        greet(line_device(lax.rem(across + d, nz)))
    for d, c in row_order:
        greet((row_target(d, c), col))

    def turn(pair):
        pltpu.make_async_copy(panels.at[pair], panels.at[pair], load_sem.at[pair]).wait()
        for tile in range(width // LANES):
            turned[pair, tile * LANES:(tile + 1) * LANES, :] = panels[pair, :, tile * LANES:(tile + 1) * LANES].T

    turn(0)
    pl.semaphore_wait(barrier, rows_n - 1 + plane - 1 + nz - 1)

    def arrival(pair, chip):
        return a2a_recv.at[0 if pair == 0 else 1 + chip]

    def a2a(pair, d, c, send):
        to = row_target(d, c)
        return remote(
            turned.at[pair, pl.ds(pl.multiple_of(to * own_cols, 8), own_cols)],
            got.at[pair, row, pl.ds(0, own_cols)],
            a2a_send.at[send], arrival(pair, z), (to, col))

    def landed(ref, semaphore):
        remote(ref, ref, core_send.at[0], semaphore, (other, col)).wait_recv()

    def left(ref, semaphore):
        remote(ref, ref, semaphore, core_recv.at[0], (other, col)).wait_send()

    first_col = col == 0
    head_core = core == 0
    carries = jnp.logical_and(head_core, col < head_pieces)
    lane = lax.broadcasted_iota(jnp.int32, (slab, LANES), 1)

    def merge(left, right, lanes):
        return (jnp.where(lanes < 64, left, pltpu.roll(right, 64, 1)),
                jnp.where(lanes < 64, pltpu.roll(left, 64, 1), right))

    to_core0 = remote(turned.at[0, pl.ds(0, slab)], head_x, core_send.at[0], core_recv.at[0], (other, col))

    def h1(p):
        return remote(head_own.at[pl.ds(pl.multiple_of(p * head_piece, 8), head_piece)], head_slot,
                      head_send.at[0], head_recv.at[0], (row, p))

    def h2(d):
        return remote(head_slot, head_ring.at[z], head_send.at[1], head_recv.at[1],
                      (lax.rem(z + d, nz) * 2 + core, col))

    def h3(k):
        return remote(head_ring, head_all.at[:, pl.ds(pl.multiple_of(col * head_piece, 8), head_piece)],
                      head_send.at[2], head_recv.at[2], (row, lax.rem(col + k, plane)))

    order = [(pair, d, c) for pair in range(2) for d, c in row_order]
    window = min(6, len(row_order) // 2)

    def issue(first, last):
        for i in range(first, min(last, len(order))):
            if window <= i < 2 * window:
                left(turned.at[0, pl.ds(0, own_cols)], a2a_send.at[i - window])
            a2a(*order[i], i if i < window else window + order[i][0]).start()

    @pl.when(jnp.logical_and(first_col, core == 1))
    def _():
        to_core0.start()

    issue(0, window)

    @pl.when(jnp.logical_and(first_col, head_core))
    def _():
        to_core0.wait_recv()
        head, head_cot = merge(turned[0, 0:slab, :], head_x[...], lane)
        head_own[...] = head
        here = pl.ds(pl.multiple_of(z * LANES, LANES), LANES)
        head_extra[...] = head * value_cot[:, here] + head_cot / values[:, here]
        loop(head_pieces, lambda p: h1(p).start(), 1)
        head_slot[...] = head[0:head_piece]

    @pl.when(jnp.logical_and(first_col, core == 1))
    def _():
        to_core0.wait_send()

    turn(1)
    got[:, :, own_cols:, :] = jnp.zeros((2, rows_n, LANES - own_cols, LANES), F32)
    for pair in range(2):
        got[pair, row, 0:own_cols, :] = turned[pair, pl.ds(pl.multiple_of(row * own_cols, 8), own_cols), :]

    @pl.when(carries)
    def _():
        @pl.when(jnp.logical_not(first_col))
        def _():
            landed(head_slot, head_recv.at[0])
        for d in line_order:
            h2(d).start()
        head_ring[z] = head_slot[...]

    issue(window, 2 * window)

    @pl.when(carries)
    def _():
        landed(head_ring.at[pl.ds(0, nz - 1)], head_recv.at[1])
        loop(plane, lambda k: h3(k).start(), 1)
        head_all[:, pl.ds(pl.multiple_of(col * head_piece, 8), head_piece), :] = head_ring[...]

    issue(2 * window, len(order))

    def a2a_sent():
        left(turned.at[0, pl.ds(0, (len(row_order) - window) * own_cols)], a2a_send.at[window])
        left(turned.at[1, pl.ds(0, len(row_order) * own_cols)], a2a_send.at[window + 1])

    sent.append(a2a_sent)

    for j in range(nz):
        here = slice(j * LANES, (j + 1) * LANES)
        column[here, :] = jnp.broadcast_to(values[:, here] * values[:, here], (LANES, LANES)).T

    def gaps(j):
        here = pl.ds(pl.multiple_of(j * LANES, LANES), LANES)
        across_values = values[:, here]
        spacing = across_values * across_values - column[...]
        factor[:, here] = spacing / (spacing * spacing + BROADEN)

    loop(nz, gaps)

    def head_sent():
        @pl.when(jnp.logical_and(first_col, head_core))
        def _():
            left(head_own.at[pl.ds(0, slab - head_piece)], head_send.at[0])

        @pl.when(carries)
        def _():
            left(head_ring.at[pl.ds(0, nz - 1)], head_send.at[1])
            left(factor.at[pl.ds(0, (plane - 1) * head_piece)], head_send.at[2])

    sent.append(head_sent)

    def through(stacked, count, high, rest, dot):
        both = dot(stacked, high)
        return both[:count] + both[count:] + dot(stacked[:count], rest)

    def prepare(pair):
        lanes = lax.broadcasted_iota(jnp.int32, (LANES, LANES), 1)

        def take(j):
            first, second = merge(got[pair, 2 * j], got[pair, 2 * j + 1], lanes)
            here = pl.ds(pl.multiple_of(j * LANES, LANES), LANES)
            if pair == 1:
                p_own[:, here] = first
            for at, value in ((0, second), (LANES, first)):
                high, rest = split(value)
                rhs[pair, at:at + LANES, here] = high
                rhs[pair, 256 + at:256 + at + LANES, here] = high
                rhs[pair, 512 + at:512 + at + LANES, here] = rest
                if pair == 1 and at == 0:
                    third[...] = third[...] + through(heads[2, :, here], slab, high, rest, dot_nt)
            for at, value in ((0, first.T), (LANES, -second.T)):
                high, rest = split(value)
                lhs[here, at:at + LANES] = high
                lhs[here, 256 + at:256 + at + LANES] = rest
                lhs[here, 512 + at:512 + at + LANES] = high

        def arrive(i):
            d = nz // 2 + ((i + 1) // 2) * (1 - 2 * (i % 2))
            j = lax.rem(z + nz - d, nz)
            if pair == 1:
                landed(got.at[pair, pl.ds(2 * j, 2), pl.ds(0, own_cols)], arrival(pair, j))
            take(j)

        if pair == 0:
            landed(got.at[pair, pl.ds(0, rows_n - 1), pl.ds(0, own_cols)], arrival(pair, z))
        else:
            landed(got.at[pair, 0, pl.ds(0, own_cols)], arrival(pair, z))
        take(z)
        loop(nz - 1, arrive)

    def set_low(value):
        high, rest = split(value)
        low[0:slab, :] = high
        low[slab:, :] = rest

    def columns(pair, j):
        here = slice(j * block, (j + 1) * block)
        right = rhs[pair, :, here]
        step = min(256, block)
        for start in range(block * j, keep, step):
            there = slice(start, start + step)
            value = factor[there, here] * dot_nn(lhs[there, :], right)
            sym_high[there, here], sym_rest[there, here] = split(value)
            if start >= block * (j + 1):
                sym_high[here, there], sym_rest[here, there] = split(value.T)
        total = through(heads[pair], slab, sym_high[:, here], sym_rest[:, here], dot_nn)
        at = LANES * pair
        outer = through(low[...], slab, right[at:at + LANES], right[512 + at:512 + at + LANES], dot_nn)
        if pair == 0:
            w_acc[:, here] = total * values[:, here] - outer / values[:, here]
            return
        total = w_acc[:, here] + total - outer
        for t in range(block // LANES):
            for h in range(2):
                for g in range(groups):
                    start = h * half + g * piece
                    w_part[h, (j * (block // LANES) + t) * groups + g] = total[start:start + piece, t * LANES:(t + 1) * LANES]

    prepare(0)

    to_core1 = remote(head_all, head_all, core_send.at[1], core_recv.at[1], (other, col))

    @pl.when(head_core)
    def _():
        @pl.when(col < head_pieces)
        def _():
            landed(head_all.at[:, pl.ds(0, slab - head_piece)], head_recv.at[2])

        @pl.when(col >= head_pieces)
        def _():
            landed(head_all, head_recv.at[2])
        to_core1.start()

    @pl.when(core == 1)
    def _():
        to_core1.wait_recv()

    def head_core_sent():
        @pl.when(head_core)
        def _():
            to_core1.wait_send()

    sent.append(head_core_sent)

    def head_parts(j):
        here = pl.ds(pl.multiple_of(j * LANES, LANES), LANES)
        head = head_all[j]
        for which, value in enumerate((head, head * values[:, here], head / values[:, here])):
            high, rest = split(value)
            heads[which, 0:slab, here] = high
            heads[which, slab:, here] = rest

    loop(nz, head_parts)
    set_low(through(heads[0], slab, rhs[0, LANES:256, :], rhs[0, 640:768, :], dot_nt))
    for j in range(keep // block):
        columns(0, j)

    @pl.when(jnp.logical_and(first_col, head_core))
    def _():
        here = pl.ds(pl.multiple_of(z * LANES, LANES), LANES)
        w_acc[:, here] = w_acc[:, here] + head_extra[...]

    third[...] = jnp.zeros((slab, LANES), F32)
    prepare(1)
    set_low(third[...])
    p_swap = remote(p_own, p_other, core_send.at[2], core_recv.at[2], (other, col))
    third_swap = remote(third.at[pl.ds(pl.multiple_of((1 - core) * half, 8), half)], third_other,
                        core_send.at[3], core_recv.at[3], (other, col))
    p_swap.start()
    third_swap.start()
    sent.extend((p_swap.wait_send, third_swap.wait_send))

    per = groups * block // LANES

    def w_swap(j):
        part = pl.ds(j * per, per)
        return remote(w_part.at[1 - core, part], w_other.at[part],
                      core_send.at[4 + j], core_recv.at[4 + j], (other, col))

    mine_now = (lax.rem(along, 2) * (nz // 2) + along // 2) * groups + x

    def rs(j, dx, i):
        t = lax.rem(along + i * 2 + lax.rem(along + j, 2), ny)
        g = lax.rem(x + dx, nx)
        q = (lax.rem(t, 2) * (nz // 2) + t // 2) * groups + g
        return remote(rs_src.at[q], rs_buf.at[me], sum_send.at[0], sum_recv.at[0], plane_device(g * ny + t))

    rs_order = sorted(
        ((dx, i) for dx in range(nx) for i in range(ny // 2)),
        key=lambda at: -min(at[0], nx - at[0]) - abs(ny / 2 - abs(2 * at[1] + 0.5 - ny / 2)))

    def scatter(j):
        w_swap(j).wait_recv()
        part = pl.ds(j * per, per)
        rs_src[part] = w_part[core, part] + w_other[part]

        for dx, i in rs_order:
            if dx or i:
                rs(j, dx, i).start()
            else:
                @pl.when(lax.rem(along + j, 2) == 1)
                def _():
                    rs(j, dx, i).start()

    for j in range(keep // block):
        columns(1, j)
        w_swap(j).start()
        sent.append(w_swap(j).wait_send)
        if j:
            scatter(j - 1)
    scatter(keep // block - 1)
    sent.append(lambda: left(rs_buf.at[pl.ds(0, plane - 1)], sum_send.at[0]))
    rs_buf[me] = rs_src[mine_now]
    landed(rs_buf.at[pl.ds(0, plane - 1)], sum_recv.at[0])
    ar_src[...] = jnp.sum(rs_buf[...], axis=0)

    for d in line_order:
        remote(ar_src, ar_buf.at[across], sum_send.at[1], sum_recv.at[1],
               line_device(lax.rem(across + d, nz))).start()
    sent.append(lambda: left(ar_buf.at[pl.ds(0, nz - 1)], sum_send.at[1]))
    ar_buf[across] = ar_src[...]
    landed(ar_buf.at[pl.ds(0, nz - 1)], sum_recv.at[1])
    ag_src[...] = jnp.sum(ar_buf[...], axis=0)

    for dx, dt in plane_order:
        remote(ag_src, w_full.at[me], sum_send.at[2], sum_recv.at[4 + x], plane_device(around(dx, dt))).start()
    sent.append(lambda: left(w_full.at[pl.ds(0, plane - 1)], sum_send.at[2]))
    w_full[me] = ag_src[...]
    p_swap.wait_recv()
    third_swap.wait_recv()
    last_high[0:LANES, :] = rhs[1, LANES:256, :]
    last_rest[0:LANES, :] = rhs[1, 640:768, :]
    high, rest = split(p_other[...])
    last_high[LANES:, :] = high
    last_rest[LANES:, :] = rest
    last_left[...] = jnp.zeros(last_left.shape, BF16)

    def send_out(i):
        return remote(out_src.at[i], out_buf.at[z], sum_send.at[3], sum_recv.at[3], (core * nz + i, col))

    def finish(i):
        dx = i + (i // 2) * (1 - 2 * (i % 2))
        g = lax.rem(x + dx, nx)

        @pl.when(dx == 0)
        def _():
            landed(w_full.at[pl.ds(0, ny - 1)], sum_recv.at[4 + g])

        @pl.when(dx != 0)
        def _():
            landed(w_full.at[pl.ds(0, ny)], sum_recv.at[4 + g])

        for zb in range(nz):
            here = slice(zb * LANES, (zb + 1) * LANES)
            high, rest = split(w_full[g * ny + 2 * (zb % (nz // 2)) + zb // (nz // 2)])
            last_left[0:piece, here] = high
            last_left[32:32 + piece, here] = rest
        both = dot_nt(last_left[...], last_high[...])
        product = both[0:piece] + both[32:32 + piece] + dot_nt(last_left[0:32, :], last_rest[...])[0:piece]
        mine = product[:, :LANES] + third[pl.ds(pl.multiple_of(core * half + g * piece, 8), piece), :]
        theirs = product[:, LANES:] + third_other[pl.ds(pl.multiple_of(g * piece, 8), piece), :]
        for c in range(2):
            to = 2 * g + c
            rows = slice(c * out_rows, (c + 1) * out_rows)
            out_src[to, core] = mine[rows]
            out_src[to, 1 - core] = theirs[rows]

            @pl.when(core * nz + to != row)
            def _():
                send_out(to).start()

    loop(nx, finish)

    keeps = core == row // nz
    own_out = pltpu.make_async_copy(out_src.at[lax.rem(row, nz)], out_buf.at[z], own_sem.at[0])

    @pl.when(keeps)
    def _():
        own_out.start()
        landed(out_buf.at[pl.ds(0, nz - 1)], sum_recv.at[3])
        left(out_src.at[pl.ds(0, nz - 1)], sum_send.at[3])
        own_out.wait()

    @pl.when(jnp.logical_not(keeps))
    def _():
        landed(out_buf, sum_recv.at[3])
        left(out_src, sum_send.at[3])

    settle()


def lay_out(own_cols, scale, blocks, out):
    for i in range(blocks.shape[0]):
        for c in range(2):
            start = (2 * i + c) * own_cols
            out[:, start:start + own_cols] = blocks[i, c, :, 0:own_cols] * scale


def body(nx, ny, nz, slab, scale, left_vecs, left_cot, right_vecs, right_cot, values, value_cot):
    rows_n, plane, keep, width = 2 * nz, nx * ny, values.shape[0], left_vecs.shape[1]
    own_cols, half = width // rows_n, slab // 2
    piece = half // (plane // nz)
    head_piece = -(-(-(-slab // plane)) // 8) * 8
    pieces = (plane, piece, LANES)
    dma = pltpu.SemaphoreType.DMA
    scratch = [
        pltpu.VMEM((2, LANES, width), F32),
        pltpu.VMEM((2, width, LANES), F32),
        pltpu.VMEM((2, rows_n, LANES, LANES), F32),
        pltpu.VMEM((keep, 768), BF16),
        pltpu.VMEM((2, 768, keep), BF16),
        pltpu.VMEM((LANES, keep), F32),
        pltpu.VMEM((LANES, keep), F32),
        pltpu.VMEM((keep, LANES), F32),
        pltpu.VMEM((keep, keep), F32),
        pltpu.VMEM((3, 2 * slab, keep), BF16),
        pltpu.VMEM((slab, LANES), F32),
        pltpu.VMEM((slab, LANES), F32),
        pltpu.VMEM((slab, LANES), F32),
        pltpu.VMEM((head_piece, LANES), F32),
        pltpu.VMEM((nz, head_piece, LANES), F32),
        pltpu.VMEM((nz, slab, LANES), F32),
        pltpu.VMEM((slab, keep), F32),
        pltpu.VMEM((2,) + pieces, F32),
        pltpu.VMEM(pieces, F32),
        pltpu.VMEM(pieces, F32),
        pltpu.VMEM(pieces, F32),
        pltpu.VMEM((piece, LANES), F32),
        pltpu.VMEM((nz, piece, LANES), F32),
        pltpu.VMEM((piece, LANES), F32),
        pltpu.VMEM(pieces, F32),
        pltpu.VMEM((keep, keep), BF16),
        pltpu.VMEM((keep, keep), BF16),
        pltpu.VMEM((2 * slab, LANES), BF16),
        pltpu.VMEM((slab, LANES), F32),
        pltpu.VMEM((half, LANES), F32),
        pltpu.VMEM((64, keep), BF16),
        pltpu.VMEM((2 * LANES, keep), BF16),
        pltpu.VMEM((2 * LANES, keep), BF16),
        pltpu.VMEM((nz, 2, slab // rows_n, LANES), F32),
        dma((2,)), dma((8,)), dma((1 + nz,)), dma((6,)), dma((6,)), dma((3,)), dma((3,)),
        dma((4,)), dma((4 + nx,)), dma((1,)),
    ]
    vmem, anywhere = pl.BlockSpec(memory_space=pltpu.VMEM), pl.BlockSpec(memory_space=pl.ANY)
    blocks = pl.pallas_call(
        functools.partial(kernel, (nx, ny, nz, piece, head_piece, slab, own_cols)),
        out_shape=jax.ShapeDtypeStruct((nz, 2, slab // rows_n, LANES), F32),
        in_specs=[anywhere] * 4 + [vmem] * 2,
        out_specs=anywhere,
        scratch_shapes=scratch,
        compiler_params=pltpu.CompilerParams(
            collective_id=0, has_side_effects=True, vmem_limit_bytes=56 * 1024 * 1024),
        cost_estimate=pl.CostEstimate(flops=12 * 2**30, bytes_accessed=2 * 2**20, transcendentals=0),
    )(left_vecs, left_cot, right_vecs, right_cot, values[None, :], value_cot[None, :])
    return pl.pallas_call(
        functools.partial(lay_out, own_cols, scale),
        out_shape=jax.ShapeDtypeStruct((slab // rows_n, width), F32),
        in_specs=[vmem], out_specs=vmem,
    )(blocks)


def build(mesh, nx, ny, nz, slab, scale):
    panel = P("row", "col")
    return jax.shard_map(
        functools.partial(body, nx, ny, nz, slab, scale), mesh=mesh,
        in_specs=(panel, panel, panel, panel, P(), P()), out_specs=panel, check_vma=False)


def solution(mesh):
    return build(mesh, 4, 8, 8, SLAB, ORDER / math.sqrt(KEEP))
```

```python
import functools
import math

import jax
import jax.numpy as jnp
from jax import lax
from jax.experimental import pallas as pl
from jax.experimental.pallas import tpu as pltpu
from jax.sharding import PartitionSpec as P

ORDER = 53248
KEEP = 1024
SLAB = 192
BROADEN = 0.0001
LANES = 128
F32 = jnp.float32
BF16 = jnp.bfloat16


def split(value):
    high = value.astype(BF16)
    return high, (value - high.astype(F32)).astype(BF16)


def dot_nn(left, right):
    return lax.dot_general(left, right, (((1,), (0,)), ((), ())), preferred_element_type=F32)


def dot_nt(left, right):
    return lax.dot_general(left, right, (((1,), (1,)), ((), ())), preferred_element_type=F32)


def kernel(geo, *refs):
    nx, ny, nz, piece, head_piece, slab, own_cols = geo
    rows_n = 2 * nz
    plane = nx * ny
    keep = nz * LANES
    half = slab // 2
    out_rows = slab // rows_n
    width = own_cols * rows_n
    head_pieces = slab // head_piece
    groups = half // piece
    block = keep // 2
    (a_in, b_in, p_in, q_in, values, value_cot, out_buf,
     panels, turned, got, lhs, rhs, p_own, p_other, column, factor,
     heads, head_own, head_x, head_extra, head_slot, head_ring, head_all,
     w_acc, w_part, w_other, rs_src, rs_buf, ar_src, ar_buf, ag_src, w_full,
     sym_high, sym_rest, low, third, third_other, last_left, last_high, last_rest, out_src,
     load_sem, a2a_send, a2a_recv, core_send, core_recv, head_send, head_recv, sum_send, sum_recv, own_sem, known) = refs

    row = lax.axis_index("row")
    col = lax.axis_index("col")
    z, core = row // 2, row % 2
    x, y = col // ny, col % ny
    other = z * 2 + 1 - core
    along = (1 - core) * y + core * z
    across = (1 - core) * z + core * y
    me = x * ny + along

    def plane_device(index):
        px, pt = index // ny, index % ny
        py = (1 - core) * pt + core * y
        pz = (1 - core) * z + core * pt
        return (pz * 2 + core, px * ny + py)

    def line_device(index):
        py = (1 - core) * y + core * index
        pz = (1 - core) * index + core * z
        return (pz * 2 + core, x * ny + py)

    def remote(src, dst, send, recv, device):
        return pltpu.make_async_remote_copy(
            src_ref=src, dst_ref=dst, send_sem=send, recv_sem=recv,
            device_id=device, device_id_type=pl.DeviceIdType.MESH)

    def loop(count, step, first=0):
        def run(i, carry):
            step(i)
            return carry
        lax.fori_loop(first, count, run, 0)

    line_order = sorted(range(1, nz), key=lambda d: -min(d, nz - d))
    plane_order = sorted(
        ((dx, dt) for dx in range(nx) for dt in range(ny) if dx or dt),
        key=lambda at: -min(at[0], nx - at[0]) - min(at[1], ny - at[1]))
    row_order = [(0, 0)] + [(d, c) for d in line_order for c in range(2)]

    def around(dx, dt):
        return lax.rem(x + dx, nx) * ny + lax.rem(along + dt, ny)

    def row_target(d, c):
        return lax.rem(z + d, nz) * 2 + c if d else other

    sent = []

    def settle():
        for step in sent:
            step()

    barrier = pltpu.get_barrier_semaphore()

    def greet(device):
        pl.semaphore_signal(barrier, inc=1, device_id=device, device_id_type=pl.DeviceIdType.MESH)

    for i, source in enumerate((a_in, b_in, p_in, q_in)):
        pltpu.make_async_copy(source, panels.at[i // 2, pl.ds(64 * (i % 2), 64)], load_sem.at[i // 2]).start()

    for d, c in row_order[1:] + row_order[:1]:
        greet((row_target(d, c), col))
    for d in line_order:
        greet((row, x * ny + lax.rem(y + d, ny)))
    for d in range(1, nx):
        greet((row, lax.rem(x + d, nx) * ny + y))

    def turn(pair):
        pltpu.make_async_copy(panels.at[pair], panels.at[pair], load_sem.at[pair]).wait()
        for tile in range(width // LANES):
            turned[pair, tile * LANES:(tile + 1) * LANES, :] = panels[pair, :, tile * LANES:(tile + 1) * LANES].T

    turn(0)
    pl.semaphore_wait(barrier, rows_n - 1 + ny - 1 + nx - 1)

    def arrival(pair, chip):
        return a2a_recv.at[0 if pair == 0 else 1 + chip]

    def a2a(pair, d, c, send):
        to = row_target(d, c)
        return remote(
            turned.at[pair, pl.ds(pl.multiple_of(to * own_cols, 8), own_cols)],
            got.at[pair, row, pl.ds(0, own_cols)],
            a2a_send.at[send], arrival(pair, z), (to, col))

    def landed(ref, semaphore):
        remote(ref, ref, core_send.at[0], semaphore, (other, col)).wait_recv()

    def left(ref, semaphore):
        remote(ref, ref, semaphore, core_recv.at[0], (other, col)).wait_send()

    first_col = col == 0
    head_core = core == 0
    carries = jnp.logical_and(head_core, col < head_pieces)
    lane = lax.broadcasted_iota(jnp.int32, (slab, LANES), 1)

    def merge(left, right, lanes):
        return (jnp.where(lanes < 64, left, pltpu.roll(right, 64, 1)),
                jnp.where(lanes < 64, pltpu.roll(left, 64, 1), right))

    to_core0 = remote(turned.at[0, pl.ds(0, slab)], head_x, core_send.at[0], core_recv.at[0], (other, col))

    def h1(p):
        return remote(head_own.at[pl.ds(pl.multiple_of(p * head_piece, 8), head_piece)], head_slot,
                      head_send.at[0], head_recv.at[0], (row, p))

    def h2(d):
        return remote(head_slot, head_ring.at[z], head_send.at[1], head_recv.at[1],
                      (lax.rem(z + d, nz) * 2 + core, col))

    def h3(k):
        return remote(head_ring, head_all.at[:, pl.ds(pl.multiple_of(col * head_piece, 8), head_piece)],
                      head_send.at[2], head_recv.at[2], (row, lax.rem(col + k, plane)))

    order = [(pair, d, c) for pair in range(2) for d, c in row_order]
    window = min(6, len(row_order) // 2)

    def issue(first, last):
        for i in range(first, min(last, len(order))):
            if window <= i < 2 * window:
                left(turned.at[0, pl.ds(0, own_cols)], a2a_send.at[i - window])
            a2a(*order[i], i if i < window else window + order[i][0]).start()

    @pl.when(jnp.logical_and(first_col, core == 1))
    def _():
        to_core0.start()

    issue(0, window)

    for d in line_order:
        pl.semaphore_signal(known, inc=1, device_id=plane_device(around(0, d)),
                            device_id_type=pl.DeviceIdType.MESH)
    turn(1)
    pl.semaphore_wait(known, ny - 1)

    @pl.when(jnp.logical_and(first_col, head_core))
    def _():
        to_core0.wait_recv()
        head, head_cot = merge(turned[0, 0:slab, :], head_x[...], lane)
        head_own[...] = head
        here = pl.ds(pl.multiple_of(z * LANES, LANES), LANES)
        head_extra[...] = head * value_cot[:, here] + head_cot / values[:, here]
        loop(head_pieces, lambda p: h1(p).start(), 1)
        head_slot[...] = head[0:head_piece]

    @pl.when(jnp.logical_and(first_col, core == 1))
    def _():
        to_core0.wait_send()

    got[:, :, own_cols:, :] = jnp.zeros((2, rows_n, LANES - own_cols, LANES), F32)
    for pair in range(2):
        got[pair, row, 0:own_cols, :] = turned[pair, pl.ds(pl.multiple_of(row * own_cols, 8), own_cols), :]

    @pl.when(carries)
    def _():
        @pl.when(jnp.logical_not(first_col))
        def _():
            landed(head_slot, head_recv.at[0])
        for d in line_order:
            h2(d).start()
        head_ring[z] = head_slot[...]

    issue(window, 2 * window)

    @pl.when(carries)
    def _():
        landed(head_ring.at[pl.ds(0, nz - 1)], head_recv.at[1])
        loop(plane, lambda k: h3(k).start(), 1)
        head_all[:, pl.ds(pl.multiple_of(col * head_piece, 8), head_piece), :] = head_ring[...]

    issue(2 * window, len(order))

    def a2a_sent():
        left(turned.at[0, pl.ds(0, (len(row_order) - window) * own_cols)], a2a_send.at[window])
        left(turned.at[1, pl.ds(0, len(row_order) * own_cols)], a2a_send.at[window + 1])

    sent.append(a2a_sent)

    for j in range(nz):
        here = slice(j * LANES, (j + 1) * LANES)
        column[here, :] = jnp.broadcast_to(values[:, here] * values[:, here], (LANES, LANES)).T

    def gaps(j):
        here = pl.ds(pl.multiple_of(j * LANES, LANES), LANES)
        across_values = values[:, here]
        spacing = across_values * across_values - column[...]
        factor[:, here] = spacing / (spacing * spacing + BROADEN)

    loop(nz, gaps)

    def head_sent():
        @pl.when(jnp.logical_and(first_col, head_core))
        def _():
            left(head_own.at[pl.ds(0, slab - head_piece)], head_send.at[0])

        @pl.when(carries)
        def _():
            left(head_ring.at[pl.ds(0, nz - 1)], head_send.at[1])
            left(factor.at[pl.ds(0, (plane - 1) * head_piece)], head_send.at[2])

    sent.append(head_sent)

    def through(stacked, count, high, rest, dot):
        both = dot(stacked, high)
        return both[:count] + both[count:] + dot(stacked[:count], rest)

    def prepare(pair):
        lanes = lax.broadcasted_iota(jnp.int32, (LANES, LANES), 1)

        def take(j):
            first, second = merge(got[pair, 2 * j], got[pair, 2 * j + 1], lanes)
            here = pl.ds(pl.multiple_of(j * LANES, LANES), LANES)
            if pair == 1:
                p_own[:, here] = first
            for at, value in ((0, second), (LANES, first)):
                high, rest = split(value)
                rhs[pair, at:at + LANES, here] = high
                rhs[pair, 256 + at:256 + at + LANES, here] = high
                rhs[pair, 512 + at:512 + at + LANES, here] = rest
                if pair == 1 and at == 0:
                    third[...] = third[...] + through(heads[2, :, here], slab, high, rest, dot_nt)
            for at, value in ((0, first.T), (LANES, -second.T)):
                high, rest = split(value)
                lhs[here, at:at + LANES] = high
                lhs[here, 256 + at:256 + at + LANES] = rest
                lhs[here, 512 + at:512 + at + LANES] = high

        def arrive(i):
            d = nz // 2 + ((i + 1) // 2) * (1 - 2 * (i % 2))
            j = lax.rem(z + nz - d, nz)
            if pair == 1:
                landed(got.at[pair, pl.ds(2 * j, 2), pl.ds(0, own_cols)], arrival(pair, j))
            take(j)

        if pair == 0:
            landed(got.at[pair, pl.ds(0, rows_n - 1), pl.ds(0, own_cols)], arrival(pair, z))
        else:
            landed(got.at[pair, 0, pl.ds(0, own_cols)], arrival(pair, z))
        take(z)
        loop(nz - 1, arrive)

    def set_low(value):
        high, rest = split(value)
        low[0:slab, :] = high
        low[slab:, :] = rest

    def columns(pair, j):
        here = slice(j * block, (j + 1) * block)
        right = rhs[pair, :, here]
        step = min(256, block)
        for start in range(block * j, keep, step):
            there = slice(start, start + step)
            value = factor[there, here] * dot_nn(lhs[there, :], right)
            sym_high[there, here], sym_rest[there, here] = split(value)
            if start >= block * (j + 1):
                sym_high[here, there], sym_rest[here, there] = split(value.T)
        total = through(heads[pair], slab, sym_high[:, here], sym_rest[:, here], dot_nn)
        at = LANES * pair
        outer = through(low[...], slab, right[at:at + LANES], right[512 + at:512 + at + LANES], dot_nn)
        if pair == 0:
            w_acc[:, here] = total * values[:, here] - outer / values[:, here]
            return
        total = w_acc[:, here] + total - outer
        for t in range(block // LANES):
            for h in range(2):
                for g in range(groups):
                    start = h * half + g * piece
                    w_part[h, (j * (block // LANES) + t) * groups + g] = total[start:start + piece, t * LANES:(t + 1) * LANES]

    prepare(0)

    to_core1 = remote(head_all, head_all, core_send.at[1], core_recv.at[1], (other, col))

    @pl.when(head_core)
    def _():
        @pl.when(col < head_pieces)
        def _():
            landed(head_all.at[:, pl.ds(0, slab - head_piece)], head_recv.at[2])

        @pl.when(col >= head_pieces)
        def _():
            landed(head_all, head_recv.at[2])
        to_core1.start()

    @pl.when(core == 1)
    def _():
        to_core1.wait_recv()

    def head_core_sent():
        @pl.when(head_core)
        def _():
            to_core1.wait_send()

    sent.append(head_core_sent)

    def head_parts(j):
        here = pl.ds(pl.multiple_of(j * LANES, LANES), LANES)
        head = head_all[j]
        for which, value in enumerate((head, head * values[:, here], head / values[:, here])):
            high, rest = split(value)
            heads[which, 0:slab, here] = high
            heads[which, slab:, here] = rest

    loop(nz, head_parts)
    set_low(through(heads[0], slab, rhs[0, LANES:256, :], rhs[0, 640:768, :], dot_nt))
    for j in range(keep // block):
        columns(0, j)

    @pl.when(jnp.logical_and(first_col, head_core))
    def _():
        here = pl.ds(pl.multiple_of(z * LANES, LANES), LANES)
        w_acc[:, here] = w_acc[:, here] + head_extra[...]

    third[...] = jnp.zeros((slab, LANES), F32)
    prepare(1)
    set_low(third[...])
    p_swap = remote(p_own, p_other, core_send.at[2], core_recv.at[2], (other, col))
    third_swap = remote(third.at[pl.ds(pl.multiple_of((1 - core) * half, 8), half)], third_other,
                        core_send.at[3], core_recv.at[3], (other, col))
    p_swap.start()
    third_swap.start()
    sent.extend((p_swap.wait_send, third_swap.wait_send))

    per = groups * block // LANES

    def w_swap(j):
        part = pl.ds(j * per, per)
        return remote(w_part.at[1 - core, part], w_other.at[part],
                      core_send.at[4 + j], core_recv.at[4 + j], (other, col))

    mine_now = (lax.rem(along, 2) * (nz // 2) + along // 2) * groups + x

    def rs(j, dx, i):
        t = lax.rem(along + i * 2 + lax.rem(along + j, 2), ny)
        g = lax.rem(x + dx, nx)
        q = (lax.rem(t, 2) * (nz // 2) + t // 2) * groups + g
        return remote(rs_src.at[q], rs_buf.at[me], sum_send.at[0], sum_recv.at[0], plane_device(g * ny + t))

    rs_order = sorted(
        ((dx, i) for dx in range(nx) for i in range(ny // 2)),
        key=lambda at: -min(at[0], nx - at[0]) - abs(ny / 2 - abs(2 * at[1] + 0.5 - ny / 2)))

    def scatter(j):
        w_swap(j).wait_recv()
        part = pl.ds(j * per, per)
        rs_src[part] = w_part[core, part] + w_other[part]

        for dx, i in rs_order:
            if dx or i:
                rs(j, dx, i).start()
            else:
                @pl.when(lax.rem(along + j, 2) == 1)
                def _():
                    rs(j, dx, i).start()

    for j in range(keep // block):
        columns(1, j)
        w_swap(j).start()
        sent.append(w_swap(j).wait_send)
        if j:
            scatter(j - 1)
    scatter(keep // block - 1)
    sent.append(lambda: left(rs_buf.at[pl.ds(0, plane - 1)], sum_send.at[0]))
    rs_buf[me] = rs_src[mine_now]
    landed(rs_buf.at[pl.ds(0, plane - 1)], sum_recv.at[0])
    ar_src[...] = jnp.sum(rs_buf[...], axis=0)

    for d in line_order:
        remote(ar_src, ar_buf.at[across], sum_send.at[1], sum_recv.at[1],
               line_device(lax.rem(across + d, nz))).start()
    sent.append(lambda: left(ar_buf.at[pl.ds(0, nz - 1)], sum_send.at[1]))
    ar_buf[across] = ar_src[...]
    landed(ar_buf.at[pl.ds(0, nz - 1)], sum_recv.at[1])
    ag_src[...] = jnp.sum(ar_buf[...], axis=0)

    for dx, dt in plane_order:
        remote(ag_src, w_full.at[me], sum_send.at[2], sum_recv.at[4 + x], plane_device(around(dx, dt))).start()
    sent.append(lambda: left(w_full.at[pl.ds(0, plane - 1)], sum_send.at[2]))
    w_full[me] = ag_src[...]
    p_swap.wait_recv()
    third_swap.wait_recv()
    last_high[0:LANES, :] = rhs[1, LANES:256, :]
    last_rest[0:LANES, :] = rhs[1, 640:768, :]
    high, rest = split(p_other[...])
    last_high[LANES:, :] = high
    last_rest[LANES:, :] = rest
    last_left[...] = jnp.zeros(last_left.shape, BF16)

    def send_out(i):
        return remote(out_src.at[i], out_buf.at[z], sum_send.at[3], sum_recv.at[3], (core * nz + i, col))

    def finish(i):
        dx = i + (i // 2) * (1 - 2 * (i % 2))
        g = lax.rem(x + dx, nx)

        @pl.when(dx == 0)
        def _():
            landed(w_full.at[pl.ds(0, ny - 1)], sum_recv.at[4 + g])

        @pl.when(dx != 0)
        def _():
            landed(w_full.at[pl.ds(0, ny)], sum_recv.at[4 + g])

        for zb in range(nz):
            here = slice(zb * LANES, (zb + 1) * LANES)
            high, rest = split(w_full[g * ny + 2 * (zb % (nz // 2)) + zb // (nz // 2)])
            last_left[0:piece, here] = high
            last_left[32:32 + piece, here] = rest
        both = dot_nt(last_left[...], last_high[...])
        product = both[0:piece] + both[32:32 + piece] + dot_nt(last_left[0:32, :], last_rest[...])[0:piece]
        mine = product[:, :LANES] + third[pl.ds(pl.multiple_of(core * half + g * piece, 8), piece), :]
        theirs = product[:, LANES:] + third_other[pl.ds(pl.multiple_of(g * piece, 8), piece), :]
        for c in range(2):
            to = 2 * g + c
            rows = slice(c * out_rows, (c + 1) * out_rows)
            out_src[to, core] = mine[rows]
            out_src[to, 1 - core] = theirs[rows]

            @pl.when(core * nz + to != row)
            def _():
                send_out(to).start()

    loop(nx, finish)

    keeps = core == row // nz
    own_out = pltpu.make_async_copy(out_src.at[lax.rem(row, nz)], out_buf.at[z], own_sem.at[0])

    @pl.when(keeps)
    def _():
        own_out.start()
        landed(out_buf.at[pl.ds(0, nz - 1)], sum_recv.at[3])
        left(out_src.at[pl.ds(0, nz - 1)], sum_send.at[3])
        own_out.wait()

    @pl.when(jnp.logical_not(keeps))
    def _():
        landed(out_buf, sum_recv.at[3])
        left(out_src, sum_send.at[3])

    settle()


def lay_out(own_cols, scale, blocks, out):
    for i in range(blocks.shape[0]):
        for c in range(2):
            start = (2 * i + c) * own_cols
            out[:, start:start + own_cols] = blocks[i, c, :, 0:own_cols] * scale


def body(nx, ny, nz, slab, scale, left_vecs, left_cot, right_vecs, right_cot, values, value_cot):
    rows_n, plane, keep, width = 2 * nz, nx * ny, values.shape[0], left_vecs.shape[1]
    own_cols, half = width // rows_n, slab // 2
    piece = half // (plane // nz)
    head_piece = -(-(-(-slab // plane)) // 8) * 8
    pieces = (plane, piece, LANES)
    dma = pltpu.SemaphoreType.DMA
    scratch = [
        pltpu.VMEM((2, LANES, width), F32),
        pltpu.VMEM((2, width, LANES), F32),
        pltpu.VMEM((2, rows_n, LANES, LANES), F32),
        pltpu.VMEM((keep, 768), BF16),
        pltpu.VMEM((2, 768, keep), BF16),
        pltpu.VMEM((LANES, keep), F32),
        pltpu.VMEM((LANES, keep), F32),
        pltpu.VMEM((keep, LANES), F32),
        pltpu.VMEM((keep, keep), F32),
        pltpu.VMEM((3, 2 * slab, keep), BF16),
        pltpu.VMEM((slab, LANES), F32),
        pltpu.VMEM((slab, LANES), F32),
        pltpu.VMEM((slab, LANES), F32),
        pltpu.VMEM((head_piece, LANES), F32),
        pltpu.VMEM((nz, head_piece, LANES), F32),
        pltpu.VMEM((nz, slab, LANES), F32),
        pltpu.VMEM((slab, keep), F32),
        pltpu.VMEM((2,) + pieces, F32),
        pltpu.VMEM(pieces, F32),
        pltpu.VMEM(pieces, F32),
        pltpu.VMEM(pieces, F32),
        pltpu.VMEM((piece, LANES), F32),
        pltpu.VMEM((nz, piece, LANES), F32),
        pltpu.VMEM((piece, LANES), F32),
        pltpu.VMEM(pieces, F32),
        pltpu.VMEM((keep, keep), BF16),
        pltpu.VMEM((keep, keep), BF16),
        pltpu.VMEM((2 * slab, LANES), BF16),
        pltpu.VMEM((slab, LANES), F32),
        pltpu.VMEM((half, LANES), F32),
        pltpu.VMEM((64, keep), BF16),
        pltpu.VMEM((2 * LANES, keep), BF16),
        pltpu.VMEM((2 * LANES, keep), BF16),
        pltpu.VMEM((nz, 2, slab // rows_n, LANES), F32),
        dma((2,)), dma((8,)), dma((1 + nz,)), dma((6,)), dma((6,)), dma((3,)), dma((3,)),
        dma((4,)), dma((4 + nx,)), dma((1,)),
        pltpu.SemaphoreType.REGULAR,
    ]
    vmem, anywhere = pl.BlockSpec(memory_space=pltpu.VMEM), pl.BlockSpec(memory_space=pl.ANY)
    blocks = pl.pallas_call(
        functools.partial(kernel, (nx, ny, nz, piece, head_piece, slab, own_cols)),
        out_shape=jax.ShapeDtypeStruct((nz, 2, slab // rows_n, LANES), F32),
        in_specs=[anywhere] * 4 + [vmem] * 2,
        out_specs=anywhere,
        scratch_shapes=scratch,
        compiler_params=pltpu.CompilerParams(
            collective_id=0, has_side_effects=True, vmem_limit_bytes=56 * 1024 * 1024),
        cost_estimate=pl.CostEstimate(flops=12 * 2**30, bytes_accessed=2 * 2**20, transcendentals=0),
    )(left_vecs, left_cot, right_vecs, right_cot, values[None, :], value_cot[None, :])
    return pl.pallas_call(
        functools.partial(lay_out, own_cols, scale),
        out_shape=jax.ShapeDtypeStruct((slab // rows_n, width), F32),
        in_specs=[vmem], out_specs=vmem,
    )(blocks)


def build(mesh, nx, ny, nz, slab, scale):
    panel = P("row", "col")
    return jax.shard_map(
        functools.partial(body, nx, ny, nz, slab, scale), mesh=mesh,
        in_specs=(panel, panel, panel, panel, P(), P()), out_specs=panel, check_vma=False)


def solution(mesh):
    return build(mesh, 4, 8, 8, SLAB, ORDER / math.sqrt(KEEP))
```

```python
import functools
import math

import jax
import jax.numpy as jnp
from jax import lax
from jax.experimental import pallas as pl
from jax.experimental.pallas import tpu as pltpu
from jax.sharding import PartitionSpec as P

ORDER = 53248
KEEP = 1024
SLAB = 192
BROADEN = 0.0001
LANES = 128
F32 = jnp.float32
BF16 = jnp.bfloat16


def split(value):
    high = value.astype(BF16)
    return high, (value - high.astype(F32)).astype(BF16)


def dot_nn(left, right):
    return lax.dot_general(left, right, (((1,), (0,)), ((), ())), preferred_element_type=F32)


def dot_nt(left, right):
    return lax.dot_general(left, right, (((1,), (1,)), ((), ())), preferred_element_type=F32)


def kernel(geo, *refs):
    nx, ny, nz, piece, head_piece, slab, own_cols = geo
    rows_n = 2 * nz
    plane = nx * ny
    keep = nz * LANES
    half = slab // 2
    out_rows = slab // rows_n
    width = own_cols * rows_n
    head_pieces = slab // head_piece
    groups = half // piece
    block = keep // 2
    (a_in, b_in, p_in, q_in, values, value_cot, out_buf,
     panels, turned, got, lhs, rhs, p_own, p_other, column, factor,
     heads, head_own, head_x, head_extra, head_slot, head_ring, head_all,
     w_acc, w_part, w_other, rs_src, rs_buf, ar_src, ar_buf, ag_src, w_full,
     sym_high, sym_rest, low, third, third_other, last_left, last_high, last_rest, out_src,
     load_sem, a2a_send, a2a_recv, core_send, core_recv, head_send, head_recv, sum_send, sum_recv, own_sem, known) = refs

    row = lax.axis_index("row")
    col = lax.axis_index("col")
    z, core = row // 2, row % 2
    x, y = col // ny, col % ny
    other = z * 2 + 1 - core
    along = (1 - core) * y + core * z
    across = (1 - core) * z + core * y
    me = x * ny + along

    def plane_device(index):
        px, pt = index // ny, index % ny
        py = (1 - core) * pt + core * y
        pz = (1 - core) * z + core * pt
        return (pz * 2 + core, px * ny + py)

    def line_device(index):
        py = (1 - core) * y + core * index
        pz = (1 - core) * index + core * z
        return (pz * 2 + core, x * ny + py)

    def remote(src, dst, send, recv, device):
        return pltpu.make_async_remote_copy(
            src_ref=src, dst_ref=dst, send_sem=send, recv_sem=recv,
            device_id=device, device_id_type=pl.DeviceIdType.MESH)

    def loop(count, step, first=0):
        def run(i, carry):
            step(i)
            return carry
        lax.fori_loop(first, count, run, 0)

    line_order = sorted(range(1, nz), key=lambda d: -min(d, nz - d))
    plane_order = sorted(
        ((dx, dt) for dx in range(nx) for dt in range(ny) if dx or dt),
        key=lambda at: -min(at[0], nx - at[0]) - min(at[1], ny - at[1]))
    row_order = [(0, 0)] + [(d, c) for d in line_order for c in range(2)]

    def around(dx, dt):
        return lax.rem(x + dx, nx) * ny + lax.rem(along + dt, ny)

    def row_target(d, c):
        return lax.rem(z + d, nz) * 2 + c if d else other

    sent = []

    def settle():
        for step in sent:
            step()

    barrier = pltpu.get_barrier_semaphore()

    def greet(device):
        pl.semaphore_signal(barrier, inc=1, device_id=device, device_id_type=pl.DeviceIdType.MESH)

    for i, source in enumerate((a_in, b_in, p_in, q_in)):
        pltpu.make_async_copy(source, panels.at[i // 2, pl.ds(64 * (i % 2), 64)], load_sem.at[i // 2]).start()

    for d, c in row_order[1:] + row_order[:1]:
        greet((row_target(d, c), col))
    for d in line_order:
        greet((row, x * ny + lax.rem(y + d, ny)))
    for d in range(1, nx):
        greet((row, lax.rem(x + d, nx) * ny + y))

    def turn(pair):
        pltpu.make_async_copy(panels.at[pair], panels.at[pair], load_sem.at[pair]).wait()
        for tile in range(width // LANES):
            turned[pair, tile * LANES:(tile + 1) * LANES, :] = panels[pair, :, tile * LANES:(tile + 1) * LANES].T

    turn(0)
    pl.semaphore_wait(barrier, rows_n - 1 + ny - 1 + nx - 1)

    def arrival(pair, chip):
        return a2a_recv.at[0 if pair == 0 else 1 + chip]

    def a2a(pair, d, c, send):
        to = row_target(d, c)
        return remote(
            turned.at[pair, pl.ds(pl.multiple_of(to * own_cols, 8), own_cols)],
            got.at[pair, row, pl.ds(0, own_cols)],
            a2a_send.at[send], arrival(pair, z), (to, col))

    def landed(ref, semaphore):
        remote(ref, ref, core_send.at[0], semaphore, (other, col)).wait_recv()

    def left(ref, semaphore):
        remote(ref, ref, semaphore, core_recv.at[0], (other, col)).wait_send()

    first_col = col == 0
    head_core = core == 0
    carries = jnp.logical_and(head_core, col < head_pieces)
    lane = lax.broadcasted_iota(jnp.int32, (slab, LANES), 1)

    def merge(left, right, lanes):
        return (jnp.where(lanes < 64, left, pltpu.roll(right, 64, 1)),
                jnp.where(lanes < 64, pltpu.roll(left, 64, 1), right))

    to_core0 = remote(turned.at[0, pl.ds(0, slab)], head_x, core_send.at[0], core_recv.at[0], (other, col))

    def h1(p):
        return remote(head_own.at[pl.ds(pl.multiple_of(p * head_piece, 8), head_piece)], head_slot,
                      head_send.at[0], head_recv.at[0], (row, p))

    def h2(d):
        return remote(head_slot, head_ring.at[z], head_send.at[1], head_recv.at[1],
                      (lax.rem(z + d, nz) * 2 + core, col))

    def h3(k):
        return remote(head_ring, head_all.at[:, pl.ds(pl.multiple_of(col * head_piece, 8), head_piece)],
                      head_send.at[2], head_recv.at[2], (row, lax.rem(col + k, plane)))

    order = [(pair, d, c) for pair in range(2) for d, c in row_order]
    window = min(6, len(row_order) // 2)

    def issue(first, last):
        for i in range(first, min(last, len(order))):
            if window <= i < 2 * window:
                left(turned.at[0, pl.ds(0, own_cols)], a2a_send.at[i - window])
            a2a(*order[i], i if i < window else window + order[i][0]).start()

    @pl.when(jnp.logical_and(first_col, core == 1))
    def _():
        to_core0.start()

    issue(0, window)

    for d in line_order:
        pl.semaphore_signal(known, inc=1, device_id=plane_device(around(0, d)),
                            device_id_type=pl.DeviceIdType.MESH)
    turn(1)
    pl.semaphore_wait(known, ny - 1)

    @pl.when(jnp.logical_and(first_col, head_core))
    def _():
        to_core0.wait_recv()
        head, head_cot = merge(turned[0, 0:slab, :], head_x[...], lane)
        head_own[...] = head
        here = pl.ds(pl.multiple_of(z * LANES, LANES), LANES)
        head_extra[...] = head * value_cot[:, here] + head_cot / values[:, here]
        loop(head_pieces, lambda p: h1(p).start(), 1)
        head_slot[...] = head[0:head_piece]

    @pl.when(jnp.logical_and(first_col, core == 1))
    def _():
        to_core0.wait_send()

    got[:, :, own_cols:, :] = jnp.zeros((2, rows_n, LANES - own_cols, LANES), F32)
    for pair in range(2):
        got[pair, row, 0:own_cols, :] = turned[pair, pl.ds(pl.multiple_of(row * own_cols, 8), own_cols), :]

    @pl.when(carries)
    def _():
        @pl.when(jnp.logical_not(first_col))
        def _():
            landed(head_slot, head_recv.at[0])
        for d in line_order:
            h2(d).start()
        head_ring[z] = head_slot[...]

    issue(window, 2 * window)

    @pl.when(carries)
    def _():
        landed(head_ring.at[pl.ds(0, nz - 1)], head_recv.at[1])
        loop(plane, lambda k: h3(k).start(), 1)
        head_all[:, pl.ds(pl.multiple_of(col * head_piece, 8), head_piece), :] = head_ring[...]

    issue(2 * window, len(order))

    def a2a_sent():
        left(turned.at[0, pl.ds(0, (len(row_order) - window) * own_cols)], a2a_send.at[window])
        left(turned.at[1, pl.ds(0, len(row_order) * own_cols)], a2a_send.at[window + 1])

    sent.append(a2a_sent)

    for j in range(nz):
        here = slice(j * LANES, (j + 1) * LANES)
        column[here, :] = jnp.broadcast_to(values[:, here] * values[:, here], (LANES, LANES)).T

    def gaps(j):
        here = pl.ds(pl.multiple_of(j * LANES, LANES), LANES)
        across_values = values[:, here]
        spacing = across_values * across_values - column[...]
        factor[:, here] = spacing / (spacing * spacing + BROADEN)

    loop(nz, gaps)

    def head_sent():
        @pl.when(jnp.logical_and(first_col, head_core))
        def _():
            left(head_own.at[pl.ds(0, slab - head_piece)], head_send.at[0])

        @pl.when(carries)
        def _():
            left(head_ring.at[pl.ds(0, nz - 1)], head_send.at[1])
            left(factor.at[pl.ds(0, (plane - 1) * head_piece)], head_send.at[2])

    sent.append(head_sent)

    def through(stacked, count, high, rest, dot):
        both = dot(stacked, high)
        return both[:count] + both[count:] + dot(stacked[:count], rest)

    def prepare(pair):
        lanes = lax.broadcasted_iota(jnp.int32, (LANES, LANES), 1)

        def take(j):
            first, second = merge(got[pair, 2 * j], got[pair, 2 * j + 1], lanes)
            here = pl.ds(pl.multiple_of(j * LANES, LANES), LANES)
            if pair == 1:
                p_own[:, here] = first
            for at, value in ((0, second), (LANES, first)):
                high, rest = split(value)
                rhs[pair, at:at + LANES, here] = high
                rhs[pair, 256 + at:256 + at + LANES, here] = high
                rhs[pair, 512 + at:512 + at + LANES, here] = rest
                if pair == 1 and at == 0:
                    third[...] = third[...] + through(heads[2, :, here], slab, high, rest, dot_nt)
            for at, value in ((0, first.T), (LANES, -second.T)):
                high, rest = split(value)
                lhs[pair, here, at:at + LANES] = high
                lhs[pair, here, 256 + at:256 + at + LANES] = rest
                lhs[pair, here, 512 + at:512 + at + LANES] = high

        def arrive(i):
            d = nz // 2 + ((i + 1) // 2) * (1 - 2 * (i % 2))
            j = lax.rem(z + nz - d, nz)
            if pair == 1:
                landed(got.at[pair, pl.ds(2 * j, 2), pl.ds(0, own_cols)], arrival(pair, j))
            take(j)

        if pair == 0:
            landed(got.at[pair, pl.ds(0, rows_n - 1), pl.ds(0, own_cols)], arrival(pair, z))
        else:
            landed(got.at[pair, 0, pl.ds(0, own_cols)], arrival(pair, z))
        take(z)
        loop(nz - 1, arrive)

    def set_low(value):
        high, rest = split(value)
        low[0:slab, :] = high
        low[slab:, :] = rest

    def symmetric(pair, j):
        here = slice(j * block, (j + 1) * block)
        right = rhs[pair, :, here]
        step = min(256, block)
        for start in range(block * j, keep, step):
            there = slice(start, start + step)
            value = factor[there, here] * dot_nn(lhs[pair, there, :], right)
            sym_high[pair, there, here], sym_rest[pair, there, here] = split(value)
            if start >= block * (j + 1):
                sym_high[pair, here, there], sym_rest[pair, here, there] = split(value.T)

    def columns(pair, j):
        here = slice(j * block, (j + 1) * block)
        right = rhs[pair, :, here]
        total = through(heads[pair], slab, sym_high[pair, :, here], sym_rest[pair, :, here], dot_nn)
        at = LANES * pair
        outer = through(low[...], slab, right[at:at + LANES], right[512 + at:512 + at + LANES], dot_nn)
        if pair == 0:
            w_acc[:, here] = total * values[:, here] - outer / values[:, here]
            return
        total = w_acc[:, here] + total - outer
        for t in range(block // LANES):
            for h in range(2):
                for g in range(groups):
                    start = h * half + g * piece
                    w_part[h, (j * (block // LANES) + t) * groups + g] = total[start:start + piece, t * LANES:(t + 1) * LANES]

    prepare(0)
    for j in range(2):
        symmetric(0, j)

    to_core1 = remote(head_all, head_all, core_send.at[1], core_recv.at[1], (other, col))

    @pl.when(head_core)
    def _():
        @pl.when(col < head_pieces)
        def _():
            landed(head_all.at[:, pl.ds(0, slab - head_piece)], head_recv.at[2])

        @pl.when(col >= head_pieces)
        def _():
            landed(head_all, head_recv.at[2])
        to_core1.start()

    @pl.when(core == 1)
    def _():
        to_core1.wait_recv()

    def head_core_sent():
        @pl.when(head_core)
        def _():
            to_core1.wait_send()

    sent.append(head_core_sent)

    def head_parts(j):
        here = pl.ds(pl.multiple_of(j * LANES, LANES), LANES)
        head = head_all[j]
        for which, value in enumerate((head, head * values[:, here], head / values[:, here])):
            high, rest = split(value)
            heads[which, 0:slab, here] = high
            heads[which, slab:, here] = rest

    loop(nz, head_parts)
    set_low(through(heads[0], slab, rhs[0, LANES:256, :], rhs[0, 640:768, :], dot_nt))
    for j in range(keep // block):
        columns(0, j)

    @pl.when(jnp.logical_and(first_col, head_core))
    def _():
        here = pl.ds(pl.multiple_of(z * LANES, LANES), LANES)
        w_acc[:, here] = w_acc[:, here] + head_extra[...]

    third[...] = jnp.zeros((slab, LANES), F32)
    prepare(1)
    set_low(third[...])
    p_swap = remote(p_own, p_other, core_send.at[2], core_recv.at[2], (other, col))
    third_swap = remote(third.at[pl.ds(pl.multiple_of((1 - core) * half, 8), half)], third_other,
                        core_send.at[3], core_recv.at[3], (other, col))
    p_swap.start()
    third_swap.start()
    sent.extend((p_swap.wait_send, third_swap.wait_send))

    per = groups * block // LANES

    def w_swap(j):
        part = pl.ds(j * per, per)
        return remote(w_part.at[1 - core, part], w_other.at[part],
                      core_send.at[4 + j], core_recv.at[4 + j], (other, col))

    mine_now = (lax.rem(along, 2) * (nz // 2) + along // 2) * groups + x

    def rs(j, dx, i):
        t = lax.rem(along + i * 2 + lax.rem(along + j, 2), ny)
        g = lax.rem(x + dx, nx)
        q = (lax.rem(t, 2) * (nz // 2) + t // 2) * groups + g
        return remote(rs_src.at[q], rs_buf.at[me], sum_send.at[0], sum_recv.at[0], plane_device(g * ny + t))

    rs_order = sorted(
        ((dx, i) for dx in range(nx) for i in range(ny // 2)),
        key=lambda at: -min(at[0], nx - at[0]) - abs(ny / 2 - abs(2 * at[1] + 0.5 - ny / 2)))

    def scatter(j):
        w_swap(j).wait_recv()
        part = pl.ds(j * per, per)
        rs_src[part] = w_part[core, part] + w_other[part]

        for dx, i in rs_order:
            if dx or i:
                rs(j, dx, i).start()
            else:
                @pl.when(lax.rem(along + j, 2) == 1)
                def _():
                    rs(j, dx, i).start()

    for j in range(keep // block):
        symmetric(1, j)
        columns(1, j)
        w_swap(j).start()
        sent.append(w_swap(j).wait_send)
        if j:
            scatter(j - 1)
    scatter(keep // block - 1)
    sent.append(lambda: left(rs_buf.at[pl.ds(0, plane - 1)], sum_send.at[0]))
    rs_buf[me] = rs_src[mine_now]
    landed(rs_buf.at[pl.ds(0, plane - 1)], sum_recv.at[0])
    ar_src[...] = jnp.sum(rs_buf[...], axis=0)

    for d in line_order:
        remote(ar_src, ar_buf.at[across], sum_send.at[1], sum_recv.at[1],
               line_device(lax.rem(across + d, nz))).start()
    sent.append(lambda: left(ar_buf.at[pl.ds(0, nz - 1)], sum_send.at[1]))
    ar_buf[across] = ar_src[...]
    landed(ar_buf.at[pl.ds(0, nz - 1)], sum_recv.at[1])
    ag_src[...] = jnp.sum(ar_buf[...], axis=0)

    for dx, dt in plane_order:
        remote(ag_src, w_full.at[me], sum_send.at[2], sum_recv.at[4 + x], plane_device(around(dx, dt))).start()
    sent.append(lambda: left(w_full.at[pl.ds(0, plane - 1)], sum_send.at[2]))
    w_full[me] = ag_src[...]
    p_swap.wait_recv()
    third_swap.wait_recv()
    last_high[0:LANES, :] = rhs[1, LANES:256, :]
    last_rest[0:LANES, :] = rhs[1, 640:768, :]
    high, rest = split(p_other[...])
    last_high[LANES:, :] = high
    last_rest[LANES:, :] = rest
    last_left[...] = jnp.zeros(last_left.shape, BF16)

    def send_out(i):
        return remote(out_src.at[i], out_buf.at[z], sum_send.at[3], sum_recv.at[3], (core * nz + i, col))

    def finish(i):
        dx = i + (i // 2) * (1 - 2 * (i % 2))
        g = lax.rem(x + dx, nx)

        @pl.when(dx == 0)
        def _():
            landed(w_full.at[pl.ds(0, ny - 1)], sum_recv.at[4 + g])

        @pl.when(dx != 0)
        def _():
            landed(w_full.at[pl.ds(0, ny)], sum_recv.at[4 + g])

        for zb in range(nz):
            here = slice(zb * LANES, (zb + 1) * LANES)
            high, rest = split(w_full[g * ny + 2 * (zb % (nz // 2)) + zb // (nz // 2)])
            last_left[0:piece, here] = high
            last_left[32:32 + piece, here] = rest
        both = dot_nt(last_left[...], last_high[...])
        product = both[0:piece] + both[32:32 + piece] + dot_nt(last_left[0:32, :], last_rest[...])[0:piece]
        mine = product[:, :LANES] + third[pl.ds(pl.multiple_of(core * half + g * piece, 8), piece), :]
        theirs = product[:, LANES:] + third_other[pl.ds(pl.multiple_of(g * piece, 8), piece), :]
        for c in range(2):
            to = 2 * g + c
            rows = slice(c * out_rows, (c + 1) * out_rows)
            out_src[to, core] = mine[rows]
            out_src[to, 1 - core] = theirs[rows]

            @pl.when(core * nz + to != row)
            def _():
                send_out(to).start()

    loop(nx, finish)

    keeps = core == row // nz
    own_out = pltpu.make_async_copy(out_src.at[lax.rem(row, nz)], out_buf.at[z], own_sem.at[0])

    @pl.when(keeps)
    def _():
        own_out.start()
        landed(out_buf.at[pl.ds(0, nz - 1)], sum_recv.at[3])
        left(out_src.at[pl.ds(0, nz - 1)], sum_send.at[3])
        own_out.wait()

    @pl.when(jnp.logical_not(keeps))
    def _():
        landed(out_buf, sum_recv.at[3])
        left(out_src, sum_send.at[3])

    settle()


def lay_out(own_cols, scale, blocks, out):
    for i in range(blocks.shape[0]):
        for c in range(2):
            start = (2 * i + c) * own_cols
            out[:, start:start + own_cols] = blocks[i, c, :, 0:own_cols] * scale


def body(nx, ny, nz, slab, scale, left_vecs, left_cot, right_vecs, right_cot, values, value_cot):
    rows_n, plane, keep, width = 2 * nz, nx * ny, values.shape[0], left_vecs.shape[1]
    own_cols, half = width // rows_n, slab // 2
    piece = half // (plane // nz)
    head_piece = -(-(-(-slab // plane)) // 8) * 8
    pieces = (plane, piece, LANES)
    dma = pltpu.SemaphoreType.DMA
    scratch = [
        pltpu.VMEM((2, LANES, width), F32),
        pltpu.VMEM((2, width, LANES), F32),
        pltpu.VMEM((2, rows_n, LANES, LANES), F32),
        pltpu.VMEM((2, keep, 768), BF16),
        pltpu.VMEM((2, 768, keep), BF16),
        pltpu.VMEM((LANES, keep), F32),
        pltpu.VMEM((LANES, keep), F32),
        pltpu.VMEM((keep, LANES), F32),
        pltpu.VMEM((keep, keep), F32),
        pltpu.VMEM((3, 2 * slab, keep), BF16),
        pltpu.VMEM((slab, LANES), F32),
        pltpu.VMEM((slab, LANES), F32),
        pltpu.VMEM((slab, LANES), F32),
        pltpu.VMEM((head_piece, LANES), F32),
        pltpu.VMEM((nz, head_piece, LANES), F32),
        pltpu.VMEM((nz, slab, LANES), F32),
        pltpu.VMEM((slab, keep), F32),
        pltpu.VMEM((2,) + pieces, F32),
        pltpu.VMEM(pieces, F32),
        pltpu.VMEM(pieces, F32),
        pltpu.VMEM(pieces, F32),
        pltpu.VMEM((piece, LANES), F32),
        pltpu.VMEM((nz, piece, LANES), F32),
        pltpu.VMEM((piece, LANES), F32),
        pltpu.VMEM(pieces, F32),
        pltpu.VMEM((2, keep, keep), BF16),
        pltpu.VMEM((2, keep, keep), BF16),
        pltpu.VMEM((2 * slab, LANES), BF16),
        pltpu.VMEM((slab, LANES), F32),
        pltpu.VMEM((half, LANES), F32),
        pltpu.VMEM((64, keep), BF16),
        pltpu.VMEM((2 * LANES, keep), BF16),
        pltpu.VMEM((2 * LANES, keep), BF16),
        pltpu.VMEM((nz, 2, slab // rows_n, LANES), F32),
        dma((2,)), dma((8,)), dma((1 + nz,)), dma((6,)), dma((6,)), dma((3,)), dma((3,)),
        dma((4,)), dma((4 + nx,)), dma((1,)),
        pltpu.SemaphoreType.REGULAR,
    ]
    vmem, anywhere = pl.BlockSpec(memory_space=pltpu.VMEM), pl.BlockSpec(memory_space=pl.ANY)
    blocks = pl.pallas_call(
        functools.partial(kernel, (nx, ny, nz, piece, head_piece, slab, own_cols)),
        out_shape=jax.ShapeDtypeStruct((nz, 2, slab // rows_n, LANES), F32),
        in_specs=[anywhere] * 4 + [vmem] * 2,
        out_specs=anywhere,
        scratch_shapes=scratch,
        compiler_params=pltpu.CompilerParams(
            collective_id=0, has_side_effects=True, vmem_limit_bytes=56 * 1024 * 1024),
        cost_estimate=pl.CostEstimate(flops=12 * 2**30, bytes_accessed=2 * 2**20, transcendentals=0),
    )(left_vecs, left_cot, right_vecs, right_cot, values[None, :], value_cot[None, :])
    return pl.pallas_call(
        functools.partial(lay_out, own_cols, scale),
        out_shape=jax.ShapeDtypeStruct((slab // rows_n, width), F32),
        in_specs=[vmem], out_specs=vmem,
    )(blocks)


def build(mesh, nx, ny, nz, slab, scale):
    panel = P("row", "col")
    return jax.shard_map(
        functools.partial(body, nx, ny, nz, slab, scale), mesh=mesh,
        in_specs=(panel, panel, panel, panel, P(), P()), out_specs=panel, check_vma=False)


def solution(mesh):
    return build(mesh, 4, 8, 8, SLAB, ORDER / math.sqrt(KEEP))
```

```python
import functools
import math

import jax
import jax.numpy as jnp
from jax import lax
from jax.experimental import pallas as pl
from jax.experimental.pallas import tpu as pltpu
from jax.sharding import PartitionSpec as P

ORDER = 53248
KEEP = 1024
SLAB = 192
BROADEN = 0.0001
LANES = 128
F32 = jnp.float32
BF16 = jnp.bfloat16


def split(value):
    high = value.astype(BF16)
    return high, (value - high.astype(F32)).astype(BF16)


def dot_nn(left, right):
    return lax.dot_general(left, right, (((1,), (0,)), ((), ())), preferred_element_type=F32)


def dot_nt(left, right):
    return lax.dot_general(left, right, (((1,), (1,)), ((), ())), preferred_element_type=F32)


def kernel(geo, *refs):
    nx, ny, nz, piece, head_piece, slab, own_cols = geo
    rows_n = 2 * nz
    plane = nx * ny
    keep = nz * LANES
    half = slab // 2
    out_rows = slab // rows_n
    width = own_cols * rows_n
    head_pieces = slab // head_piece
    groups = half // piece
    block = keep // 2
    (a_in, b_in, p_in, q_in, values, value_cot, out_buf,
     panels, turned, got, lhs, rhs, p_own, p_other, column, factor,
     heads, head_own, head_x, head_extra, head_slot, head_ring, head_all,
     w_acc, w_part, w_other, rs_src, rs_buf, ar_src, ar_buf, ag_src, w_full,
     sym_high, sym_rest, low, third, third_other, last_left, last_high, last_rest, out_src,
     load_sem, a2a_send, a2a_recv, core_send, core_recv, head_send, head_recv, sum_send, sum_recv, own_sem, known) = refs

    row = lax.axis_index("row")
    col = lax.axis_index("col")
    z, core = row // 2, row % 2
    x, y = col // ny, col % ny
    other = z * 2 + 1 - core
    along = (1 - core) * y + core * z
    across = (1 - core) * z + core * y
    me = x * ny + along

    def plane_device(index):
        px, pt = index // ny, index % ny
        py = (1 - core) * pt + core * y
        pz = (1 - core) * z + core * pt
        return (pz * 2 + core, px * ny + py)

    def line_device(index):
        py = (1 - core) * y + core * index
        pz = (1 - core) * index + core * z
        return (pz * 2 + core, x * ny + py)

    def remote(src, dst, send, recv, device):
        return pltpu.make_async_remote_copy(
            src_ref=src, dst_ref=dst, send_sem=send, recv_sem=recv,
            device_id=device, device_id_type=pl.DeviceIdType.MESH)

    def loop(count, step, first=0):
        def run(i, carry):
            step(i)
            return carry
        lax.fori_loop(first, count, run, 0)

    line_order = sorted(range(1, nz), key=lambda d: -min(d, nz - d))
    plane_order = sorted(
        ((dx, dt) for dx in range(nx) for dt in range(ny) if dx or dt),
        key=lambda at: -min(at[0], nx - at[0]) - min(at[1], ny - at[1]))
    row_order = [(0, 0)] + [(d, c) for d in line_order for c in range(2)]

    def around(dx, dt):
        return lax.rem(x + dx, nx) * ny + lax.rem(along + dt, ny)

    def row_target(d, c):
        return lax.rem(z + d, nz) * 2 + c if d else other

    sent = []

    def settle():
        for step in sent:
            step()

    barrier = pltpu.get_barrier_semaphore()

    def greet(device):
        pl.semaphore_signal(barrier, inc=1, device_id=device, device_id_type=pl.DeviceIdType.MESH)

    for i, source in enumerate((a_in, b_in, p_in, q_in)):
        pltpu.make_async_copy(source, panels.at[i // 2, pl.ds(64 * (i % 2), 64)], load_sem.at[i // 2]).start()

    for d, c in row_order[1:] + row_order[:1]:
        greet((row_target(d, c), col))
    for d in line_order:
        greet((row, x * ny + lax.rem(y + d, ny)))
    for d in range(1, nx):
        greet((row, lax.rem(x + d, nx) * ny + y))

    def turn(pair):
        pltpu.make_async_copy(panels.at[pair], panels.at[pair], load_sem.at[pair]).wait()
        for tile in range(width // LANES):
            turned[pair, tile * LANES:(tile + 1) * LANES, :] = panels[pair, :, tile * LANES:(tile + 1) * LANES].T

    turn(0)
    pl.semaphore_wait(barrier, rows_n - 1 + ny - 1 + nx - 1)

    def arrival(pair, chip):
        return a2a_recv.at[0 if pair == 0 else 1 + chip]

    def a2a(pair, d, c, send):
        to = row_target(d, c)
        return remote(
            turned.at[pair, pl.ds(pl.multiple_of(to * own_cols, 8), own_cols)],
            got.at[pair, row, pl.ds(0, own_cols)],
            a2a_send.at[send], arrival(pair, z), (to, col))

    def landed(ref, semaphore):
        remote(ref, ref, core_send.at[0], semaphore, (other, col)).wait_recv()

    def left(ref, semaphore):
        remote(ref, ref, semaphore, core_recv.at[0], (other, col)).wait_send()

    first_col = col == 0
    head_core = core == 0
    carries = jnp.logical_and(head_core, col < head_pieces)
    lane = lax.broadcasted_iota(jnp.int32, (slab, LANES), 1)

    def merge(left, right, lanes):
        return (jnp.where(lanes < 64, left, pltpu.roll(right, 64, 1)),
                jnp.where(lanes < 64, pltpu.roll(left, 64, 1), right))

    to_core0 = remote(turned.at[0, pl.ds(0, slab)], head_x, core_send.at[0], core_recv.at[0], (other, col))

    def h1(p):
        return remote(head_own.at[pl.ds(pl.multiple_of(p * head_piece, 8), head_piece)], head_slot,
                      head_send.at[0], head_recv.at[0], (row, p))

    def h2(d):
        return remote(head_slot, head_ring.at[z], head_send.at[1], head_recv.at[1],
                      (lax.rem(z + d, nz) * 2 + core, col))

    def h3(k):
        return remote(head_ring, head_all.at[:, pl.ds(pl.multiple_of(col * head_piece, 8), head_piece)],
                      head_send.at[2], head_recv.at[2], (row, lax.rem(col + k, plane)))

    order = [(pair, d, c) for pair in range(2) for d, c in row_order]
    window = min(6, len(row_order) // 2)

    def issue(first, last):
        for i in range(first, min(last, len(order))):
            if window <= i < 2 * window:
                left(turned.at[0, pl.ds(0, own_cols)], a2a_send.at[i - window])
            a2a(*order[i], i if i < window else window + order[i][0]).start()

    @pl.when(jnp.logical_and(first_col, core == 1))
    def _():
        to_core0.start()

    issue(0, window)

    for d in line_order:
        pl.semaphore_signal(known, inc=1, device_id=plane_device(around(0, d)),
                            device_id_type=pl.DeviceIdType.MESH)
    turn(1)
    pl.semaphore_wait(known, ny - 1)

    @pl.when(jnp.logical_and(first_col, head_core))
    def _():
        to_core0.wait_recv()
        head, head_cot = merge(turned[0, 0:slab, :], head_x[...], lane)
        head_own[...] = head
        here = pl.ds(pl.multiple_of(z * LANES, LANES), LANES)
        head_extra[...] = head * value_cot[:, here] + head_cot / values[:, here]
        loop(head_pieces, lambda p: h1(p).start(), 1)
        head_slot[...] = head[0:head_piece]

    @pl.when(jnp.logical_and(first_col, core == 1))
    def _():
        to_core0.wait_send()

    got[:, :, own_cols:, :] = jnp.zeros((2, rows_n, LANES - own_cols, LANES), F32)
    for pair in range(2):
        got[pair, row, 0:own_cols, :] = turned[pair, pl.ds(pl.multiple_of(row * own_cols, 8), own_cols), :]

    @pl.when(carries)
    def _():
        @pl.when(jnp.logical_not(first_col))
        def _():
            landed(head_slot, head_recv.at[0])
        for d in line_order:
            h2(d).start()
        head_ring[z] = head_slot[...]

    issue(window, 2 * window)

    @pl.when(carries)
    def _():
        landed(head_ring.at[pl.ds(0, nz - 1)], head_recv.at[1])
        loop(plane, lambda k: h3(k).start(), 1)
        head_all[:, pl.ds(pl.multiple_of(col * head_piece, 8), head_piece), :] = head_ring[...]

    issue(2 * window, len(order))

    def a2a_sent():
        left(turned.at[0, pl.ds(0, (len(row_order) - window) * own_cols)], a2a_send.at[window])
        left(turned.at[1, pl.ds(0, len(row_order) * own_cols)], a2a_send.at[window + 1])

    sent.append(a2a_sent)

    for j in range(nz):
        here = slice(j * LANES, (j + 1) * LANES)
        column[here, :] = jnp.broadcast_to(values[:, here] * values[:, here], (LANES, LANES)).T

    def gaps(j):
        here = pl.ds(pl.multiple_of(j * LANES, LANES), LANES)
        across_values = values[:, here]
        spacing = across_values * across_values - column[...]
        factor[:, here] = spacing / (spacing * spacing + BROADEN)

    loop(nz, gaps)

    def head_sent():
        @pl.when(jnp.logical_and(first_col, head_core))
        def _():
            left(head_own.at[pl.ds(0, slab - head_piece)], head_send.at[0])

        @pl.when(carries)
        def _():
            left(head_ring.at[pl.ds(0, nz - 1)], head_send.at[1])
            left(factor.at[pl.ds(0, (plane - 1) * head_piece)], head_send.at[2])

    sent.append(head_sent)

    def through(stacked, count, high, rest, dot):
        both = dot(stacked, high)
        return both[:count] + both[count:] + dot(stacked[:count], rest)

    def prepare(pair):
        lanes = lax.broadcasted_iota(jnp.int32, (LANES, LANES), 1)

        def take(j):
            first, second = merge(got[pair, 2 * j], got[pair, 2 * j + 1], lanes)
            here = pl.ds(pl.multiple_of(j * LANES, LANES), LANES)
            if pair == 1:
                p_own[:, here] = first
            for at, value in ((0, second), (LANES, first)):
                high, rest = split(value)
                rhs[pair, at:at + LANES, here] = high
                rhs[pair, 256 + at:256 + at + LANES, here] = high
                rhs[pair, 512 + at:512 + at + LANES, here] = rest
                if pair == 1 and at == 0:
                    third[...] = third[...] + through(heads[2, :, here], slab, high, rest, dot_nt)
            for at, value in ((0, first.T), (LANES, -second.T)):
                high, rest = split(value)
                lhs[pair, here, at:at + LANES] = high
                lhs[pair, here, 256 + at:256 + at + LANES] = rest
                lhs[pair, here, 512 + at:512 + at + LANES] = high

        def arrive(i):
            d = nz // 2 + ((i + 1) // 2) * (1 - 2 * (i % 2))
            j = lax.rem(z + nz - d, nz)
            if pair == 1:
                landed(got.at[pair, pl.ds(2 * j, 2), pl.ds(0, own_cols)], arrival(pair, j))
            take(j)

        if pair == 0:
            landed(got.at[pair, pl.ds(0, rows_n - 1), pl.ds(0, own_cols)], arrival(pair, z))
        else:
            landed(got.at[pair, 0, pl.ds(0, own_cols)], arrival(pair, z))
        take(z)
        loop(nz - 1, arrive)

    def set_low(value):
        high, rest = split(value)
        low[0:slab, :] = high
        low[slab:, :] = rest

    def symmetric(pair, j):
        here = slice(j * block, (j + 1) * block)
        right = rhs[pair, :, here]
        step = min(256, block)
        for start in range(block * j, keep, step):
            there = slice(start, start + step)
            value = factor[there, here] * dot_nn(lhs[pair, there, :], right)
            sym_high[pair, there, here], sym_rest[pair, there, here] = split(value)
            if start >= block * (j + 1):
                sym_high[pair, here, there], sym_rest[pair, here, there] = split(value.T)

    def columns(pair, j):
        here = slice(j * block, (j + 1) * block)
        right = rhs[pair, :, here]
        total = through(heads[pair], slab, sym_high[pair, :, here], sym_rest[pair, :, here], dot_nn)
        at = LANES * pair
        outer = through(low[...], slab, right[at:at + LANES], right[512 + at:512 + at + LANES], dot_nn)
        if pair == 0:
            w_acc[:, here] = total * values[:, here] - outer / values[:, here]
            return
        total = w_acc[:, here] + total - outer
        for t in range(block // LANES):
            for h in range(2):
                for g in range(groups):
                    start = h * half + g * piece
                    w_part[h, (j * (block // LANES) + t) * groups + g] = total[start:start + piece, t * LANES:(t + 1) * LANES]

    prepare(0)
    for j in range(2):
        symmetric(0, j)

    to_core1 = remote(head_all, head_all, core_send.at[1], core_recv.at[1], (other, col))

    @pl.when(head_core)
    def _():
        @pl.when(col < head_pieces)
        def _():
            landed(head_all.at[:, pl.ds(0, slab - head_piece)], head_recv.at[2])

        @pl.when(col >= head_pieces)
        def _():
            landed(head_all, head_recv.at[2])
        to_core1.start()

    @pl.when(core == 1)
    def _():
        to_core1.wait_recv()

    def head_core_sent():
        @pl.when(head_core)
        def _():
            to_core1.wait_send()

    sent.append(head_core_sent)

    def head_parts(j):
        here = pl.ds(pl.multiple_of(j * LANES, LANES), LANES)
        head = head_all[j]
        for which, value in enumerate((head, head * values[:, here], head / values[:, here])):
            high, rest = split(value)
            heads[which, 0:slab, here] = high
            heads[which, slab:, here] = rest

    loop(nz, head_parts)
    set_low(through(heads[0], slab, rhs[0, LANES:256, :], rhs[0, 640:768, :], dot_nt))
    for j in range(keep // block):
        columns(0, j)

    @pl.when(jnp.logical_and(first_col, head_core))
    def _():
        here = pl.ds(pl.multiple_of(z * LANES, LANES), LANES)
        w_acc[:, here] = w_acc[:, here] + head_extra[...]

    third[...] = jnp.zeros((slab, LANES), F32)
    prepare(1)
    set_low(third[...])
    p_swap = remote(p_own, p_other, core_send.at[2], core_recv.at[2], (other, col))
    third_swap = remote(third.at[pl.ds(pl.multiple_of((1 - core) * half, 8), half)], third_other,
                        core_send.at[3], core_recv.at[3], (other, col))
    p_swap.start()
    third_swap.start()
    sent.extend((p_swap.wait_send, third_swap.wait_send))

    per = groups * block // LANES

    def w_swap(j):
        part = pl.ds(j * per, per)
        return remote(w_part.at[1 - core, part], w_other.at[part],
                      core_send.at[4 + j], core_recv.at[4 + j], (other, col))

    mine_now = (lax.rem(along, 2) * (nz // 2) + along // 2) * groups + x

    def rs(j, dx, i):
        t = lax.rem(along + i * 2 + lax.rem(along + j, 2), ny)
        g = lax.rem(x + dx, nx)
        q = (lax.rem(t, 2) * (nz // 2) + t // 2) * groups + g
        return remote(rs_src.at[q], rs_buf.at[me], sum_send.at[0], sum_recv.at[0], plane_device(g * ny + t))

    rs_order = sorted(
        ((dx, i) for dx in range(nx) for i in range(ny // 2)),
        key=lambda at: -min(at[0], nx - at[0]) - abs(ny / 2 - abs(2 * at[1] + 0.5 - ny / 2)))

    def scatter(j):
        w_swap(j).wait_recv()
        part = pl.ds(j * per, per)
        rs_src[part] = w_part[core, part] + w_other[part]

        for dx, i in rs_order:
            if dx or i:
                rs(j, dx, i).start()
            else:
                @pl.when(lax.rem(along + j, 2) == 1)
                def _():
                    rs(j, dx, i).start()

    for j in range(keep // block):
        symmetric(1, j)
        columns(1, j)
        w_swap(j).start()
        sent.append(w_swap(j).wait_send)
        if j:
            scatter(j - 1)
    scatter(keep // block - 1)
    sent.append(lambda: left(rs_buf.at[pl.ds(0, plane - 1)], sum_send.at[0]))
    rs_buf[me] = rs_src[mine_now]
    landed(rs_buf.at[pl.ds(0, plane - 1)], sum_recv.at[0])
    ar_src[...] = jnp.sum(rs_buf[...], axis=0)

    for d in line_order:
        remote(ar_src, ar_buf.at[across], sum_send.at[1], sum_recv.at[1],
               line_device(lax.rem(across + d, nz))).start()
    sent.append(lambda: left(ar_buf.at[pl.ds(0, nz - 1)], sum_send.at[1]))
    ar_buf[across] = ar_src[...]
    landed(ar_buf.at[pl.ds(0, nz - 1)], sum_recv.at[1])
    ag_src[...] = jnp.sum(ar_buf[...], axis=0)

    for dx, dt in plane_order:
        remote(ag_src, w_full.at[me], sum_send.at[2], sum_recv.at[4 + x], plane_device(around(dx, dt))).start()
    sent.append(lambda: left(w_full.at[pl.ds(0, plane - 1)], sum_send.at[2]))
    w_full[me] = ag_src[...]
    p_swap.wait_recv()
    third_swap.wait_recv()
    last_high[0:LANES, :] = rhs[1, LANES:256, :]
    last_rest[0:LANES, :] = rhs[1, 640:768, :]
    high, rest = split(p_other[...])
    last_high[LANES:, :] = high
    last_rest[LANES:, :] = rest

    def send_out(i):
        return remote(out_src.at[i], out_buf.at[z], sum_send.at[3], sum_recv.at[3], (core * nz + i, col))

    def finish(i):
        dx = i + (i // 2) * (1 - 2 * (i % 2))
        g = lax.rem(x + dx, nx)

        @pl.when(dx == 0)
        def _():
            landed(w_full.at[pl.ds(0, ny - 1)], sum_recv.at[4 + g])

        @pl.when(dx != 0)
        def _():
            landed(w_full.at[pl.ds(0, ny)], sum_recv.at[4 + g])

        for zb in range(nz):
            here = slice(zb * LANES, (zb + 1) * LANES)
            part = w_full[g * ny + 2 * (zb % (nz // 2)) + zb // (nz // 2)]
            last_left[0:32, here], last_left[32:64, here] = split(jnp.pad(part, ((0, 32 - piece), (0, 0))))
        both = dot_nt(last_left[...], last_high[...])
        product = both[0:piece] + both[32:32 + piece] + dot_nt(last_left[0:32, :], last_rest[...])[0:piece]
        mine = product[:, :LANES] + third[pl.ds(pl.multiple_of(core * half + g * piece, 8), piece), :]
        theirs = product[:, LANES:] + third_other[pl.ds(pl.multiple_of(g * piece, 8), piece), :]
        for c in range(2):
            to = 2 * g + c
            rows = slice(c * out_rows, (c + 1) * out_rows)
            out_src[to, core] = mine[rows]
            out_src[to, 1 - core] = theirs[rows]

            @pl.when(core * nz + to != row)
            def _():
                send_out(to).start()

    loop(nx, finish)

    keeps = core == row // nz
    own_out = pltpu.make_async_copy(out_src.at[lax.rem(row, nz)], out_buf.at[z], own_sem.at[0])

    @pl.when(keeps)
    def _():
        own_out.start()
        landed(out_buf.at[pl.ds(0, nz - 1)], sum_recv.at[3])
        left(out_src.at[pl.ds(0, nz - 1)], sum_send.at[3])
        own_out.wait()

    @pl.when(jnp.logical_not(keeps))
    def _():
        landed(out_buf, sum_recv.at[3])
        left(out_src, sum_send.at[3])

    settle()


def lay_out(own_cols, scale, blocks, out):
    for i in range(blocks.shape[0]):
        for c in range(2):
            start = (2 * i + c) * own_cols
            out[:, start:start + own_cols] = blocks[i, c, :, 0:own_cols] * scale


def body(nx, ny, nz, slab, scale, left_vecs, left_cot, right_vecs, right_cot, values, value_cot):
    rows_n, plane, keep, width = 2 * nz, nx * ny, values.shape[0], left_vecs.shape[1]
    own_cols, half = width // rows_n, slab // 2
    piece = half // (plane // nz)
    head_piece = -(-(-(-slab // plane)) // 8) * 8
    pieces = (plane, piece, LANES)
    dma = pltpu.SemaphoreType.DMA
    scratch = [
        pltpu.VMEM((2, LANES, width), F32),
        pltpu.VMEM((2, width, LANES), F32),
        pltpu.VMEM((2, rows_n, LANES, LANES), F32),
        pltpu.VMEM((2, keep, 768), BF16),
        pltpu.VMEM((2, 768, keep), BF16),
        pltpu.VMEM((LANES, keep), F32),
        pltpu.VMEM((LANES, keep), F32),
        pltpu.VMEM((keep, LANES), F32),
        pltpu.VMEM((keep, keep), F32),
        pltpu.VMEM((3, 2 * slab, keep), BF16),
        pltpu.VMEM((slab, LANES), F32),
        pltpu.VMEM((slab, LANES), F32),
        pltpu.VMEM((slab, LANES), F32),
        pltpu.VMEM((head_piece, LANES), F32),
        pltpu.VMEM((nz, head_piece, LANES), F32),
        pltpu.VMEM((nz, slab, LANES), F32),
        pltpu.VMEM((slab, keep), F32),
        pltpu.VMEM((2,) + pieces, F32),
        pltpu.VMEM(pieces, F32),
        pltpu.VMEM(pieces, F32),
        pltpu.VMEM(pieces, F32),
        pltpu.VMEM((piece, LANES), F32),
        pltpu.VMEM((nz, piece, LANES), F32),
        pltpu.VMEM((piece, LANES), F32),
        pltpu.VMEM(pieces, F32),
        pltpu.VMEM((2, keep, keep), BF16),
        pltpu.VMEM((2, keep, keep), BF16),
        pltpu.VMEM((2 * slab, LANES), BF16),
        pltpu.VMEM((slab, LANES), F32),
        pltpu.VMEM((half, LANES), F32),
        pltpu.VMEM((64, keep), BF16),
        pltpu.VMEM((2 * LANES, keep), BF16),
        pltpu.VMEM((2 * LANES, keep), BF16),
        pltpu.VMEM((nz, 2, slab // rows_n, LANES), F32),
        dma((2,)), dma((8,)), dma((1 + nz,)), dma((6,)), dma((6,)), dma((3,)), dma((3,)),
        dma((4,)), dma((4 + nx,)), dma((1,)),
        pltpu.SemaphoreType.REGULAR,
    ]
    vmem, anywhere = pl.BlockSpec(memory_space=pltpu.VMEM), pl.BlockSpec(memory_space=pl.ANY)
    blocks = pl.pallas_call(
        functools.partial(kernel, (nx, ny, nz, piece, head_piece, slab, own_cols)),
        out_shape=jax.ShapeDtypeStruct((nz, 2, slab // rows_n, LANES), F32),
        in_specs=[anywhere] * 4 + [vmem] * 2,
        out_specs=anywhere,
        scratch_shapes=scratch,
        compiler_params=pltpu.CompilerParams(
            collective_id=0, has_side_effects=True, vmem_limit_bytes=56 * 1024 * 1024),
        cost_estimate=pl.CostEstimate(flops=12 * 2**30, bytes_accessed=2 * 2**20, transcendentals=0),
    )(left_vecs, left_cot, right_vecs, right_cot, values[None, :], value_cot[None, :])
    return pl.pallas_call(
        functools.partial(lay_out, own_cols, scale),
        out_shape=jax.ShapeDtypeStruct((slab // rows_n, width), F32),
        in_specs=[vmem], out_specs=vmem,
    )(blocks)


def build(mesh, nx, ny, nz, slab, scale):
    panel = P("row", "col")
    return jax.shard_map(
        functools.partial(body, nx, ny, nz, slab, scale), mesh=mesh,
        in_specs=(panel, panel, panel, panel, P(), P()), out_specs=panel, check_vma=False)


def solution(mesh):
    return build(mesh, 4, 8, 8, SLAB, ORDER / math.sqrt(KEEP))
```
